128 devices in a mesh: gx: 16 (over y, x_hi, core), gy: 8 (over x_lo, z).
Axes of the slice: x: 4 (x_hi: 2, x_lo: 2; x = x_hi * 2 + x_lo), y: 4, z: 4, core: 2. Of those that a mesh axis runs over, the one named last changes fastest.
Arguments:
- atom_cells: int32 [3, 4, 64, 1024], P(None, None, 'gx', 'gy'), may hold values from 0 to 511, as said below
- atom_frac: float32 [3, 4, 64, 1024], P(None, None, 'gx', 'gy'), may hold values from 0 to 1
- species: int32 [4, 64, 1024], P(None, 'gx', 'gy'), may hold values from 0 to 1
- w_first: float32 [2, 32, 15], replicated, may hold values from -1 to 1
- b_first: float32 [2, 15], replicated, may hold values from -3 to 3
- w_second: float32 [2, 15, 15], replicated, may hold values from -1.5 to 1.5
- b_second: float32 [2, 15], replicated, may hold values from -3 to 3
- w_out: float32 [2, 15, 2], replicated, may hold values from -1.5 to 1.5
- b_out: float32 [2, 2], replicated, may hold values from -4 to 4
Outputs:
- atom_energy: float32 [4, 64, 1024], P(None, 'gx', 'gy')
- atom_force: float32 [3, 4, 64, 1024], P(None, None, 'gx', 'gy')
- atom_charge: float32 [4, 64, 1024], P(None, 'gx', 'gy')
The draws below stay inside these ranges and needn't reach their ends.
Inputs may be any that keep to these rules, and one draw needn't show every extreme that they name: `atom_cells`: each atom lies in its block: along x cells 8 bx to 8 bx + 7, along y likewise with by, along z cells 8 (bz + 1) to 8 (bz + 2) - 1; every block holds exactly 16 atoms.
All inputs are finite; a program needn't handle non-finite values.
Results may differ from the reference program's by a relative error of at most 0.0003.
Values sent between devices are 32-bit elements; how exact they have to be, the bound alone decides.
No kernel may reach another device: no remote copies, remote signals or barrier semaphores. Data moves between devices by JAX's collectives and lax.ppermute only.
A program may use at most 192 MiB of HBM per device.

```python
import jax
import jax.numpy as jnp
from jax import lax

NX = 512
NY = 512
NZ = 256
BLOCK = 8
SLOTS = 16
ZBLOCKS = 4
RADIAL = 16
SPECIES = 2
NEURONS = 15
XBLOCKS = 64
YBLOCKS = 64
ZROWS = 35


def draw_atom_cells(key, part):
    key = jax.random.fold_in(key, 7)
    offsets = jax.random.randint(key, (3, ZBLOCKS, XBLOCKS, YBLOCKS, SLOTS), 0, BLOCK, dtype=jnp.int32)
    extent = (ZBLOCKS, XBLOCKS, YBLOCKS, SLOTS)
    layer_index = jnp.arange(ZBLOCKS, dtype=jnp.int32).reshape(ZBLOCKS, 1, 1, 1)
    column = jnp.arange(XBLOCKS, dtype=jnp.int32).reshape(1, XBLOCKS, 1, 1)
    lane_index = jnp.arange(YBLOCKS, dtype=jnp.int32).reshape(1, 1, YBLOCKS, 1)
    corner = jnp.stack([jnp.broadcast_to(column * BLOCK, extent), jnp.broadcast_to(lane_index * BLOCK, extent), jnp.broadcast_to((layer_index + 1) * BLOCK, extent)])
    return (corner + offsets).reshape(3, ZBLOCKS, XBLOCKS, YBLOCKS * SLOTS)


def plant(values, key, low, high):
    shape = values.shape
    spot = [jax.random.randint(jax.random.fold_in(key, axis), (), 0, shape[axis]) for axis in range(len(shape))]
    values = values.at[tuple(spot)].set(low)
    longest = shape.index(max(shape))
    spot[longest] = (spot[longest] + 1) % shape[longest]
    return values.at[tuple(spot)].set(high)


def shard_levels(own_key, shape, cuts, low, high):
    level = 1.0
    for dim, blocks in cuts:
        draws = jax.random.uniform(jax.random.fold_in(jax.random.fold_in(own_key, 6), dim), (blocks,), jnp.float32, low / len(cuts), high / len(cuts))
        level = level * jnp.repeat(jnp.exp(draws), shape[dim] // blocks).reshape((-1,) + (1,) * (len(shape) - 1 - dim))
    return level


def noise(key, shape, scale, reach, kind=jnp.bfloat16):
    entries = jax.random.normal(key, shape, jnp.float32) * scale
    return jnp.minimum(jnp.maximum(entries, -reach), reach).astype(kind)


def setup_inputs(seed: int = 0) -> dict:
    key_of = jax.random.split(jax.random.key(seed), 10)
    atom_cells = draw_atom_cells(jax.random.fold_in(key_of[9], 71), 0)
    atom_frac = jnp.clip(1.0 * jax.random.uniform(key_of[1], (3, ZBLOCKS, XBLOCKS, YBLOCKS * SLOTS), jnp.float32) ** shard_levels(key_of[1], (3, ZBLOCKS, XBLOCKS, YBLOCKS * SLOTS), ((2, 16), (3, 8)), -0.2, 0.2), 0.0, 1.0)
    species = plant(jax.random.randint(key_of[2], (ZBLOCKS, XBLOCKS, YBLOCKS * SLOTS), 0, SPECIES), jax.random.fold_in(key_of[2], 1), 0, SPECIES - 1).astype(jnp.int32)
    w_first = noise(key_of[3], (SPECIES, SPECIES * RADIAL, NEURONS), (SPECIES * RADIAL) ** -0.5, 1.0, jnp.float32)
    b_first = noise(key_of[4], (SPECIES, NEURONS), 0.5, 3.0, jnp.float32)
    w_second = noise(key_of[5], (SPECIES, NEURONS, NEURONS), NEURONS ** -0.5, 1.5, jnp.float32)
    b_second = noise(key_of[6], (SPECIES, NEURONS), 0.5, 3.0, jnp.float32)
    w_out = noise(key_of[7], (SPECIES, NEURONS, 2), NEURONS ** -0.5, 1.5, jnp.float32)
    b_out = noise(key_of[8], (SPECIES, 2), 1.0, 4.0, jnp.float32)
    return dict(atom_cells=atom_cells, atom_frac=atom_frac, species=species, w_first=w_first, b_first=b_first, w_second=w_second, b_second=b_second, w_out=w_out, b_out=b_out)


EWALD_BETA = 1.0
far_cell = -100000


def spline(fraction):
    remain = 1.0 - fraction
    square = fraction * fraction
    cube_term = square * fraction
    weights = jnp.stack([remain * remain * remain / 6.0,
                         (3.0 * cube_term - 6.0 * square + 4.0) / 6.0,
                         (-3.0 * cube_term + 3.0 * square + 3.0 * fraction + 1.0) / 6.0,
                         cube_term / 6.0])
    slopes = jnp.stack([-0.5 * remain * remain,
                        0.5 * (3.0 * square - 4.0 * fraction),
                        0.5 * (-3.0 * square + 2.0 * fraction + 1.0),
                        0.5 * square])
    return weights, slopes


def stencil(local_cell, values):
    length = BLOCK + 3
    places = jnp.arange(length, dtype=jnp.int32).reshape((length,) + (1,) * local_cell.ndim)
    summed = jnp.zeros((length,) + local_cell.shape, jnp.float32)
    for offset in range(4):
        summed = summed + jnp.where(places == local_cell[None] + offset, values[offset][None], jnp.float32(0.0))
    return summed


def wrap_gap(spacing, period):
    spacing = jnp.where(spacing > period // 2, spacing - period, spacing)
    return jnp.where(spacing < -(period // 2), spacing + period, spacing)


def neighbours(tensor, width_x, width_y):
    layers = tensor.shape[-4] - 2
    pieces = []
    for shift_z in range(3):
        for shift_x in range(3):
            for shift_y in range(3):
                pieces.append(tensor[..., shift_z:shift_z + layers, shift_x:shift_x + width_x, shift_y:shift_y + width_y, :])
    return jnp.concatenate(pieces, axis=-1)


def pair_terms(own_cells, own_frac, near_cells, near_frac, near_kinds):
    gap_list = []
    for component in range(3):
        cell_gap = near_cells[component][..., None, :] - own_cells[component][..., :, None]
        if component == 0:
            cell_gap = wrap_gap(cell_gap, NX)
        if component == 1:
            cell_gap = wrap_gap(cell_gap, NY)
        gap_list.append(cell_gap.astype(jnp.float32) + (near_frac[component][..., None, :] - own_frac[component][..., :, None]))
    ratio_sq = (gap_list[0] * gap_list[0] + gap_list[1] * gap_list[1] + gap_list[2] * gap_list[2]) / float(BLOCK * BLOCK)
    row_index = jnp.arange(SLOTS, dtype=jnp.int32)[:, None]
    col_index = jnp.arange(27 * SLOTS, dtype=jnp.int32)[None, :]
    keep_mask = col_index != row_index + 13 * SLOTS
    remain = 1.0 - ratio_sq
    smooth = jnp.where(keep_mask & (ratio_sq < 1.0), remain * remain, jnp.float32(0.0))
    argument = jnp.minimum(2.0 * ratio_sq - 1.0, 1.0)
    masked = [jnp.where(near_kinds[..., None, :] == species_index, smooth, jnp.float32(0.0)) for species_index in range(SPECIES)]
    previous = jnp.ones_like(argument)
    current = argument
    features = [[] for species_index in range(SPECIES)]
    for degree in range(RADIAL):
        if degree == 0:
            chebyshev = previous
        elif degree == 1:
            chebyshev = current
        else:
            chebyshev = 2.0 * argument * current - previous
            previous = current
            current = chebyshev
        for species_index in range(SPECIES):
            features[species_index].append(jnp.sum(masked[species_index] * chebyshev, axis=-1) / SLOTS)
    return jnp.stack([item_value for group_list in features for item_value in group_list], axis=0)


def describe(ext_cells, ext_frac, ext_kinds, groups):
    layers = ext_cells.shape[1]
    width_x = ext_cells.shape[2] - 2
    width_y = ext_cells.shape[3] - 2
    padding = ((0, 0), (1, 1), (0, 0), (0, 0), (0, 0))
    near_cells = neighbours(jnp.pad(ext_cells, padding, constant_values=far_cell), width_x, width_y)
    near_frac = neighbours(jnp.pad(ext_frac, padding), width_x, width_y)
    near_kinds = neighbours(jnp.pad(ext_kinds, padding[1:]), width_x, width_y)
    own_cells = ext_cells[:, :, 1:-1, 1:-1, :]
    own_frac = ext_frac[:, :, 1:-1, 1:-1, :]
    per_group = layers * width_x * width_y // groups

    def grouped(tensor):
        return jnp.moveaxis(tensor.reshape(tensor.shape[:-4] + (groups, per_group, tensor.shape[-1])), -3, 0)

    def layer_terms(inputs):
        return pair_terms(inputs[0], inputs[1], inputs[2], inputs[3], inputs[4])

    result = lax.map(layer_terms, (grouped(own_cells), grouped(own_frac), grouped(near_cells), grouped(near_frac), grouped(near_kinds)))
    return jnp.moveaxis(result, 0, 1).reshape(SPECIES * RADIAL, layers * width_x * width_y * SLOTS)


def network(features, species_ids, w_first, b_first, w_second, b_second, w_out, b_out):
    highest = lax.Precision.HIGHEST
    result = jnp.zeros((2, features.shape[1]), jnp.float32)
    for species_index in range(SPECIES):
        first_layer = jnp.tanh(jnp.dot(w_first[species_index].T, features, precision=highest, preferred_element_type=jnp.float32) + b_first[species_index][:, None])
        second = jnp.tanh(jnp.dot(w_second[species_index].T, first_layer, precision=highest, preferred_element_type=jnp.float32) + b_second[species_index][:, None])
        output = jnp.dot(w_out[species_index].T, second, precision=highest, preferred_element_type=jnp.float32) + b_out[species_index][:, None]
        result = result + jnp.where(species_ids[None, :] == species_index, output, jnp.float32(0.0))
    return result


def charge_regions(cell_ids, fraction, charge):
    local_cell = jnp.remainder(cell_ids, BLOCK)
    weights, slopes = spline(fraction)
    along_x = stencil(local_cell[0], weights[:, 0])
    along_y = stencil(local_cell[1], weights[:, 1])
    along_z = stencil(local_cell[2], weights[:, 2]) * charge[None]
    return jnp.einsum('xbefa,ybefa,zbefa->befxyz', along_x, along_y, along_z, precision=lax.Precision.HIGHEST)


def fold_blocks(regions, block_axis, region_axis, keep_tail):
    shifted_axes = jnp.moveaxis(regions, (block_axis, region_axis), (-2, -1))
    core_part = shifted_axes[..., :BLOCK]
    tail_part = shifted_axes[..., BLOCK:]
    leading = [(0, 0)] * (tail_part.ndim - 2)
    tail_part = jnp.pad(tail_part, leading + [(0, 0), (0, BLOCK - 3)])
    if keep_tail:
        core_part = jnp.pad(core_part, leading + [(0, 1), (0, 0)])
        tail_part = jnp.pad(tail_part, leading + [(1, 0), (0, 0)])
    else:
        tail_part = jnp.pad(tail_part, leading + [(1, 0), (0, 0)])[..., :-1, :]
    combined = core_part + tail_part
    return combined.reshape(combined.shape[:-2] + (combined.shape[-2] * BLOCK,))


def spread_grid(regions, width_x, width_y):
    folded = fold_blocks(regions, 1, 3, False)
    folded = fold_blocks(folded, 1, 2, False)
    folded = fold_blocks(folded, 0, 1, True)
    return folded[BLOCK + 1:BLOCK + 1 + width_x, BLOCK + 1:BLOCK + 1 + width_y, :ZROWS]


def cut_regions(tensor, dim_index, block_count, first_index):
    shifted_axes = jnp.moveaxis(tensor, dim_index, -1)
    needed = first_index + BLOCK * (block_count + 1) - shifted_axes.shape[-1]
    if needed > 0:
        shifted_axes = jnp.pad(shifted_axes, [(0, 0)] * (shifted_axes.ndim - 1) + [(0, needed)])
    core_part = shifted_axes[..., first_index:first_index + BLOCK * block_count].reshape(shifted_axes.shape[:-1] + (block_count, BLOCK))
    tail_part = shifted_axes[..., first_index + BLOCK:first_index + BLOCK * (block_count + 1)].reshape(shifted_axes.shape[:-1] + (block_count, BLOCK))[..., :3]
    return jnp.concatenate([core_part, tail_part], axis=-1)


def potential_regions(padded, count_x, count_y):
    pieces = cut_regions(padded, 0, count_x, 1)
    pieces = cut_regions(pieces, 0, count_y, 1)
    pieces = cut_regions(pieces, 0, ZBLOCKS, 0)
    return jnp.transpose(pieces, (4, 0, 2, 1, 3, 5))


def interpolate(regions, cell_ids, fraction):
    highest = lax.Precision.HIGHEST
    local_cell = jnp.remainder(cell_ids, BLOCK)
    weights, slopes = spline(fraction)
    along_x = stencil(local_cell[0], weights[:, 0])
    along_y = stencil(local_cell[1], weights[:, 1])
    along_z = stencil(local_cell[2], weights[:, 2])
    slope_x = stencil(local_cell[0], slopes[:, 0])
    slope_y = stencil(local_cell[1], slopes[:, 1])
    slope_z = stencil(local_cell[2], slopes[:, 2])
    inner_sum = jnp.einsum('befxyz,zbefa->befxya', regions, along_z, precision=highest)
    inner_slope = jnp.einsum('befxyz,zbefa->befxya', regions, slope_z, precision=highest)
    potential = jnp.einsum('befxya,xbefa,ybefa->befa', inner_sum, along_x, along_y, precision=highest)
    gradient = jnp.stack([jnp.einsum('befxya,xbefa,ybefa->befa', inner_sum, slope_x, along_y, precision=highest),
                          jnp.einsum('befxya,xbefa,ybefa->befa', inner_sum, along_x, slope_y, precision=highest),
                          jnp.einsum('befxya,xbefa,ybefa->befa', inner_slope, along_x, along_y, precision=highest)])
    return potential, gradient


def influence(wave_z):
    def axis_terms(wave_index, length):
        signed = jnp.where(wave_index > length // 2, wave_index - length, wave_index).astype(jnp.float32) / length
        smooth = 2.0 / 3.0 + jnp.cos((2.0 * jnp.pi / length) * wave_index.astype(jnp.float32)) / 3.0
        return signed * signed, smooth * smooth

    square_z, factor_z = axis_terms(wave_z, NZ)
    square_x, factor_x = axis_terms(jnp.arange(NX, dtype=jnp.int32), NX)
    square_y, factor_y = axis_terms(jnp.arange(NY, dtype=jnp.int32), NY)
    wave_sq = square_z[:, None, None] + square_x[None, :, None] + square_y[None, None, :]
    spread = factor_z[:, None, None] * factor_x[None, :, None] * factor_y[None, None, :]
    safe_sq = jnp.where(wave_sq > 0.0, wave_sq, 1.0)
    raw_value = jnp.exp(-(jnp.pi / EWALD_BETA) ** 2 * safe_sq) / (jnp.pi * float(NX * NY * NZ) * safe_sq * spread)
    return jnp.where(wave_sq > 0.0, raw_value, jnp.float32(0.0))


def periodic_cycle(tensor, axis_x, axis_y):
    for dim_index in (axis_x, axis_y):
        extent = tensor.shape[dim_index]
        last_block = lax.slice_in_dim(tensor, extent - 1, extent, axis=dim_index)
        first_block = lax.slice_in_dim(tensor, 0, 1, axis=dim_index)
        tensor = jnp.concatenate([last_block, tensor, first_block], axis=dim_index)
    return tensor


def reference(atom_cells, atom_frac, species, w_first, b_first, w_second, b_second, w_out, b_out):
    cell_ids = atom_cells.reshape(3, ZBLOCKS, XBLOCKS, YBLOCKS, SLOTS)
    fraction = atom_frac.reshape(3, ZBLOCKS, XBLOCKS, YBLOCKS, SLOTS)
    species_ids = species.reshape(ZBLOCKS, XBLOCKS, YBLOCKS, SLOTS)
    cycle_cells = periodic_cycle(cell_ids, 2, 3)
    cycle_frac = periodic_cycle(fraction, 2, 3)
    cycle_kinds = periodic_cycle(species_ids, 1, 2)
    features = describe(cycle_cells, cycle_frac, cycle_kinds, ZBLOCKS * XBLOCKS)
    outputs = network(features, species_ids.reshape(-1), w_first, b_first, w_second, b_second, w_out, b_out)
    outputs = outputs.reshape(2, ZBLOCKS, XBLOCKS, YBLOCKS, SLOTS)
    short_energy = outputs[0]
    charge = outputs[1]
    cycle_charge = periodic_cycle(charge, 1, 2)
    charge_grid = spread_grid(charge_regions(cycle_cells, cycle_frac, cycle_charge), NX, NY)
    full_grid = jnp.pad(charge_grid, ((0, 0), (0, 0), (BLOCK - 1, NZ - BLOCK + 1 - ZROWS)))
    filter_values = jnp.transpose(influence(jnp.arange(NZ, dtype=jnp.int32)), (1, 2, 0))
    potential_grid = jnp.real(jnp.fft.ifftn(filter_values * jnp.fft.fftn(full_grid))) * float(NX * NY * NZ)
    potential_rows = potential_grid[:, :, BLOCK - 1:BLOCK - 1 + ZROWS]
    padded = jnp.pad(potential_rows, ((2, 2), (2, 2), (0, 0)), mode="wrap")
    regions = potential_regions(padded, XBLOCKS, YBLOCKS)
    potential, gradient = interpolate(regions, cell_ids, fraction)
    energy = short_energy + 0.5 * charge * potential
    atom_force = -charge[None] * gradient
    return (energy.reshape(ZBLOCKS, XBLOCKS, YBLOCKS * SLOTS),
            atom_force.reshape(3, ZBLOCKS, XBLOCKS, YBLOCKS * SLOTS),
            charge.reshape(ZBLOCKS, XBLOCKS, YBLOCKS * SLOTS))
```

```python
import functools

import jax
import jax.numpy as jnp
import ml_dtypes
import numpy as np
from jax import lax
from jax.experimental import pallas as pl
from jax.experimental.pallas import tpu as pltpu
from jax.sharding import PartitionSpec as P

NX = 512
NY = 512
NZ = 256
BLOCK = 8
SLOTS = 16
ZBLOCKS = 4
RADIAL = 16
SPECIES = 2
NEURONS = 15
ZROWS = 35
ZPAD = 40
PLANES = 128
EWALD_BETA = 1.0
LANES = 128
PATCH_ROWS = 18
WIRE_ROWS = PATCH_ROWS + 1
NT = (((1,), (1,)), ((), ()))
NN = (((1,), (0,)), ((), ()))
TN = (((0,), (0,)), ((), ()))
VMEM_BYTES = 40 * 1024 * 1024


def high_low(table):
    high = table.astype(ml_dtypes.bfloat16)
    low = (table - high.astype(np.float64)).astype(ml_dtypes.bfloat16)
    return high, low


def split(value):
    high = value.astype(jnp.bfloat16)
    low = (value - high.astype(jnp.float32)).astype(jnp.bfloat16)
    return high, low


def dot(left, right, dims=NN):
    return lax.dot_general(left, right, dims, preferred_element_type=jnp.float32)


def dot3(left, right, dims=NN):
    return (
        dot(left[0], right[0], dims) + dot(left[0], right[1], dims) + dot(left[1], right[0], dims)
    )


def cas(left, right, length):
    angle = 2.0 * np.pi / length * (np.outer(left, right) % length)
    return np.cos(angle) + np.sin(angle)


def wave_order(length):
    half = length // 2
    return np.concatenate([np.arange(half + 1), length - np.arange(1, half)])


def axis_factor(wave, length):
    signed = np.where(wave > length // 2, wave - length, wave) / length
    smooth = 2.0 / 3.0 + np.cos(2.0 * np.pi / length * wave) / 3.0
    return signed**2, np.exp(-((np.pi / EWALD_BETA) ** 2) * signed**2) / smooth**2


def spline_weight(distance):
    away = jnp.abs(distance)
    outer = jnp.maximum(2.0 - away, 0.0)
    inner = jnp.maximum(1.0 - away, 0.0)
    return (outer * outer * outer - 4.0 * (inner * inner * inner)) * (1.0 / 6.0)


def spline_both(distance):
    away = jnp.abs(distance)
    outer = jnp.maximum(2.0 - away, 0.0)
    inner = jnp.maximum(1.0 - away, 0.0)
    outer_sq = outer * outer
    inner_sq = inner * inner
    weight = (outer_sq * outer - 4.0 * (inner_sq * inner)) * (1.0 / 6.0)
    slope = 0.5 * outer_sq - 2.0 * inner_sq
    return weight, jnp.where(distance > 0.0, slope, -slope)


def iota(shape, dim):
    return lax.broadcasted_iota(jnp.int32, shape, dim)


def row_vector(rows):
    return jnp.concatenate(
        [rows[bz * 4 + bx : bz * 4 + bx + 1, :] for bx in range(4) for bz in range(4)], axis=1
    )


def z_distance(pos_z):
    shape = (ZPAD, pos_z.shape[1])
    layer = (iota(shape, 1) // LANES) % ZBLOCKS
    return (iota(shape, 0) - 8 * layer - 1).astype(jnp.float32) - 8.0 * pos_z


def y_distance(pos_y, shape, cell):
    block = (iota(shape, 1) % LANES) // SLOTS
    return (cell - 1 - 8 * block).astype(jnp.float32) - 8.0 * pos_y


def atoms_kernel(
    ext_ref,
    left_ref,
    right_ref,
    packed_ref,
    basis_ref,
    short_ref,
    charge_ref,
    wire_ref,
    near_ref,
    feature_ref,
    weight_ref,
    bias_ref,
):
    lane = iota((LANES, LANES), 1)
    own = ext_ref[...].reshape(LANES, LANES)
    left = left_ref[...].reshape(LANES, LANES)
    right = right_ref[...].reshape(LANES, LANES)
    shifted = [
        jnp.where(lane < SLOTS, pltpu.roll(left, SLOTS, 1), pltpu.roll(own, SLOTS, 1)),
        own,
        jnp.where(
            lane >= LANES - SLOTS,
            pltpu.roll(right, LANES - SLOTS, 1),
            pltpu.roll(own, LANES - SLOTS, 1),
        ),
    ]
    far = jnp.full((4, LANES), 100.0, jnp.float32)
    for dx in range(3):
        for dy in range(3):
            n = dx * 3 + dy
            for c in range(4):
                offset = float((dx - 1, dy - 1, 0, 0)[c])
                for bz in range(ZBLOCKS):
                    row = (c * ZBLOCKS + bz) * 8 + dx
                    near_ref[n, c, 4 + 4 * bz : 8 + 4 * bz, :] = shifted[dy][row : row + 4, :] + offset
                near_ref[n, c, 0:4, :] = far
                near_ref[n, c, 20:24, :] = far

    lane8 = iota((8, LANES), 1)
    for half in range(2):
        mine = [near_ref[4, c, 4 + 8 * half : 12 + 8 * half, :] for c in range(3)]

        def body(n, sums):
            sums = list(sums)
            keep = jnp.where(n == 4, 0.0, 1.0).astype(jnp.float32)
            for dz in range(3):
                near = [
                    near_ref[n, c, 4 * dz + 8 * half : 4 * dz + 8 * half + 8, :] for c in range(4)
                ]
                mine_z = mine[2] - float(dz - 1)
                for turn in range(SLOTS):
                    if turn == 0:
                        got = near
                    else:
                        index = (lane8 & (LANES - SLOTS)) | ((lane8 + turn) & (SLOTS - 1))
                        got = [jnp.take_along_axis(v, index, axis=1) for v in near]
                    gx = got[0] - mine[0]
                    gy = got[1] - mine[1]
                    gz = got[2] - mine_z
                    kind = got[3]
                    remain = jnp.maximum(1.0 - (gx * gx + gy * gy + gz * gz), 0.0)
                    if turn == 0 and dz == 1:
                        remain = remain * keep
                    twice = 2.0 - 4.0 * remain
                    previous = remain * remain
                    current = 0.5 * twice * previous
                    for k in range(RADIAL):
                        if k == 0:
                            term = previous
                        elif k == 1:
                            term = current
                        else:
                            term = twice * current - previous
                            previous, current = current, term
                        sums[k] = sums[k] + term
                        sums[RADIAL + k] = sums[RADIAL + k] + term * kind
            return tuple(sums)

        zero = jnp.zeros((8, LANES), jnp.float32)
        sums = lax.fori_loop(0, 9, body, (zero,) * (2 * RADIAL))
        for k in range(RADIAL):
            one = sums[RADIAL + k] * (1.0 / SLOTS)
            feature_ref[k, 8 * half : 8 * half + 8, :] = sums[k] * (1.0 / SLOTS) - one
            feature_ref[RADIAL + k, 8 * half : 8 * half + 8, :] = one

    features = jnp.concatenate(
        [feature_ref[:, bz * 4 + bx, :] for bx in range(4) for bz in range(4)], axis=1
    )
    weight_ref[...] = jnp.zeros(weight_ref.shape, jnp.float32)
    bias_ref[...] = jnp.zeros(bias_ref.shape, jnp.float32)
    for s in range(SPECIES):
        at = s * 16
        row = s * 72
        weight_ref[0, :, at : at + NEURONS] = packed_ref[row : row + 32, :NEURONS]
        weight_ref[1, at : at + NEURONS, at : at + NEURONS] = packed_ref[row + 32 : row + 47, :NEURONS]
        weight_ref[2, at : at + NEURONS, 2 * s : 2 * s + 2] = packed_ref[row + 48 : row + 63, :2]
        bias_ref[0:1, at : at + NEURONS] = packed_ref[row + 64 : row + 65, :NEURONS]
        bias_ref[1:2, at : at + NEURONS] = packed_ref[row + 65 : row + 66, :NEURONS]
        bias_ref[2:3, 2 * s : 2 * s + 2] = packed_ref[row + 66 : row + 67, :2]
    diagonal = iota((LANES, LANES), 0) == iota((LANES, LANES), 1)

    def layer(n, x, height):
        bias = jnp.sum(
            jnp.where(diagonal[:height], bias_ref[n : n + 1, :], 0.0), axis=1, keepdims=True
        )
        full = lax.dot_general(
            weight_ref[n, :, :height], x, TN, precision=lax.Precision.HIGHEST, preferred_element_type=jnp.float32
        )
        return full + bias

    rows = [near_ref[4, c, 4:20, :] for c in range(4)]
    pos_x, pos_y, pos_z, kinds = [row_vector(r) for r in rows]
    answers = layer(2, jnp.tanh(layer(1, jnp.tanh(layer(0, features, 32)), 32)), 8)
    answer = jnp.where(kinds == 0.0, answers[0:2, :], answers[2:4, :])
    charge = answer[1:2, :]
    for bx in range(4):
        for bz in range(4):
            at = (bx * 4 + bz) * LANES
            short_ref[bz, bx : bx + 1, :] = answer[0:1, at : at + LANES]
            charge_ref[bz, bx : bx + 1, :] = charge[:, at : at + LANES]

    along_z = split(spline_weight(z_distance(pos_z)))
    waves = dot3(split(basis_ref[...]), along_z) * charge
    waves_high, waves_low = split(waves)

    per = 4 * LANES
    carry = [None, None]
    tail = None
    for bx in range(4):
        cut = slice(bx * per, (bx + 1) * per)
        ux, uy = 8.0 * pos_x[:, cut], pos_y[:, cut]
        waves_cut = (waves_high[:, cut], waves_low[:, cut])
        weight_y = spline_weight(y_distance(uy, (64, per), iota((64, per), 0)))
        weight_x = spline_weight((iota((16, per), 0) - 1).astype(jnp.float32) - ux)
        for pair in range(6):
            product = jnp.concatenate(
                [weight_y * weight_x[2 * pair + h : 2 * pair + h + 1, :] for h in range(2)], axis=0
            )
            plane = dot3(waves_cut, split(product), NT)
            if pair < 2 and bx > 0:
                plane = plane + carry[pair]
            if pair >= 4 and bx < 3:
                carry[pair - 4] = plane
            else:
                wire_ref[pl.ds(4 * bx + pair, PLANES, stride=WIRE_ROWS), :] = plane
        place = iota((LANES, per), 0)
        tail_x = spline_weight((place // 3 - 1 - 8 * bx).astype(jnp.float32) - ux)
        tail_y = spline_weight(y_distance(uy, (LANES, per), 64 + place % 3))
        more = dot3(waves_cut, split(tail_x * tail_y), NT)
        tail = more if tail is None else tail + more
    wire_ref[pl.ds(PATCH_ROWS, PLANES, stride=WIRE_ROWS), :] = tail


def pack_weights(w_first, b_first, w_second, b_second, w_out, b_out):
    def wide(part, height):
        return jnp.pad(part, ((0, 0), (0, height - part.shape[1]), (0, LANES - part.shape[2])))

    biases = jnp.stack([b_first, b_second, jnp.pad(b_out, ((0, 0), (0, NEURONS - 2)))], axis=1)
    parts = [wide(w_first, 32), wide(w_second, 16), wide(w_out, 16), wide(biases, 8)]
    return jnp.concatenate(parts, axis=1).reshape(-1, LANES)


def atoms_call(ext, left, right, packed):
    wave = np.arange(PLANES)
    basis = np.zeros((PLANES, ZPAD))
    basis[:, :ZROWS] = cas(wave, np.arange(ZROWS), PLANES)
    f32 = jnp.float32
    return pl.pallas_call(
        atoms_kernel,
        out_shape=(
            jax.ShapeDtypeStruct((4, 4, LANES), f32),
            jax.ShapeDtypeStruct((4, 4, LANES), f32),
            jax.ShapeDtypeStruct((PLANES * WIRE_ROWS, LANES), f32),
        ),
        scratch_shapes=[
            pltpu.VMEM((9, 4, 24, LANES), f32),
            pltpu.VMEM((SPECIES * RADIAL, 16, LANES), f32),
            pltpu.VMEM((3, 32, LANES), f32),
            pltpu.VMEM((8, LANES), f32),
        ],
        compiler_params=pltpu.CompilerParams(vmem_limit_bytes=VMEM_BYTES),
        name="atoms",
    )(ext, left, right, packed, basis.astype(np.float32))


def filter_kernel(terms_ref, squares_ref, row_ref, column_ref, out_ref):
    half = NX // 2
    count = NZ // 4

    def series(square):
        total = None
        for t in range(1, count + 1, 4):
            near = [square + squares_ref[t + n] for n in range(4)]
            parts = [
                (
                    terms_ref[t + n] * near[n + 1] + terms_ref[t + n + 1] * near[n],
                    near[n] * near[n + 1],
                )
                for n in (0, 2)
            ]
            part = (parts[0][0] * parts[1][1] + parts[1][0] * parts[0][1]) / (
                parts[0][1] * parts[1][1]
            )
            total = part if total is None else total + part
        even = square + squares_ref[0]
        extra = terms_ref[0] / jnp.where(even > 0.0, even, 1.0)
        return total + jnp.where(even > 0.0, extra, 0.0)

    edge = series(row_ref[0:8, :] + 0.25) * row_ref[8:16, :] * column_ref[half : half + 8, 1:2]
    edge = edge[0:1, :]
    edge_low, edge_corner = edge[:, :half], edge[:, half : half + 1]
    first_lane = iota((16, half), 1) == 0

    def body(n, _):
        at = pl.multiple_of(n * 16, 16)
        column = column_ref[pl.ds(at, 16), :]
        value = series(row_ref[0:1, :half] + column[:, 0:1]) * row_ref[8:9, :half] * column[:, 1:2]
        row = at + iota((16, half), 0)
        mirror = jnp.sum(
            jnp.where(row == iota((16, half), 1), edge_low, 0.0), axis=1, keepdims=True
        )
        right = jnp.where(first_lane, mirror, value)
        out_ref[pl.ds(at, 16), :half] = value
        out_ref[pl.ds(at, 16), half:] = right
        out_ref[pl.ds(half + at, 16), :half] = jnp.where(row == 0, edge_low, value)
        corner = jnp.where(first_lane, edge_corner, edge_low)
        out_ref[pl.ds(half + at, 16), half:] = jnp.where(row == 0, corner, right)
        return 0

    lax.fori_loop(0, half // 16, body, 0)


def filter_tables():
    plane = np.arange(PLANES)[:, None]
    odd = np.arange(1, NZ // 2, 2)
    gaps = np.arange(-(PLANES // 2) + 1, PLANES // 2 + 1)
    window = np.cos(2.0 * np.pi / PLANES * plane * gaps) @ np.cos(
        2.0 * np.pi / NZ * gaps[:, None] * odd
    )
    even = 2 * np.minimum(plane, PLANES - plane)
    wave = np.concatenate([even, np.broadcast_to(odd, (PLANES, odd.size))], axis=1)
    square, factor = axis_factor(wave, NZ)
    count = np.concatenate([np.full((PLANES, 1), float(PLANES)), 2.0 * window], axis=1)
    terms = count * factor / (np.pi * NX * NY * NZ * PLANES)
    return terms.astype(np.float32), square.astype(np.float32)


def filter_call(plane):
    terms, squares = filter_tables()
    square, factor = axis_factor(wave_order(NX), NX)
    row = np.repeat(np.stack([square, factor]), 8, axis=0).astype(np.float32)
    column = np.stack([square, factor], axis=1).astype(np.float32)
    smem = pl.BlockSpec(memory_space=pltpu.SMEM)
    vmem = pl.BlockSpec(memory_space=pltpu.VMEM)
    return pl.pallas_call(
        filter_kernel,
        out_shape=jax.ShapeDtypeStruct((NX, NY), jnp.float32),
        in_specs=[smem, smem, vmem, vmem],
        compiler_params=pltpu.CompilerParams(vmem_limit_bytes=VMEM_BYTES),
        cost_estimate=pl.CostEstimate(flops=20_000_000, bytes_accessed=1 << 20, transcendentals=0),
        name="filter",
    )(
        lax.dynamic_index_in_dim(jnp.asarray(terms), plane, 0, keepdims=False),
        lax.dynamic_index_in_dim(jnp.asarray(squares), plane, 0, keepdims=False),
        row,
        column,
    )


def plane_kernel(
    count_x,
    count_y,
    wire_ref,
    filter_ref,
    square_ref,
    wide_ref,
    out_ref,
    grid_high,
    grid_low,
    result_ref,
):
    stride = count_y * WIRE_ROWS
    pairs = count_y // 2
    lane = iota((count_x, LANES), 1)
    low_half = lane < 64
    tails = [wire_ref[pl.ds(j * WIRE_ROWS + PATCH_ROWS, count_x, stride=stride), :] for j in range(count_y)]
    for m in range(pairs):
        before = tails[(2 * m - 1) % count_y]
        between = tails[2 * m]
        for r in range(PATCH_ROWS):
            one = wire_ref[pl.ds(2 * m * WIRE_ROWS + r, count_x, stride=stride), :]
            two = wire_ref[pl.ds((2 * m + 1) * WIRE_ROWS + r, count_x, stride=stride), :]
            for h in range(2):
                x = 2 * r + h
                if h == 0:
                    value = jnp.where(low_half, one, pltpu.roll(two, 64, 1))
                else:
                    value = jnp.where(low_half, pltpu.roll(one, 64, 1), two)
                first = pltpu.roll(before, (LANES - 3 * x) % LANES, 1) if x else before
                second = pltpu.roll(between, (LANES + 64 - 3 * x) % LANES, 1)
                value = value + jnp.where(lane < 3, first, 0.0)
                value = value + jnp.where((lane >= 64) & (lane < 67), second, 0.0)
                high, low = split(value)
                at = x * count_x
                grid_high[at : at + count_x, m * LANES : (m + 1) * LANES] = high
                grid_low[at : at + count_x, m * LANES : (m + 1) * LANES] = low

    rows = 2 * PATCH_ROWS * count_x

    def table(n, height):
        return square_ref[n : n + height, :], square_ref[n + height : n + 2 * height, :]

    step = split(dot3((grid_high[...], grid_low[...]), table(0, NY)))
    spectrum = dot3((wide_ref[:NX, :], wide_ref[NX:, :]), step) * filter_ref[...]
    mean = spectrum[0:1, 0:1]
    first = (iota((8, NY), 0) == 0) & (iota((8, NY), 1) == 0)
    spectrum = jnp.concatenate([jnp.where(first, 0.0, spectrum[:8]), spectrum[8:]], axis=0)
    step = split(dot3(table(4 * NY, rows), split(spectrum)))
    result_ref[...] = dot3(step, table(2 * NY, NY))

    for j in range(count_y):
        m = j // 2
        for r in range(PATCH_ROWS):
            even = result_ref[2 * r * count_x : (2 * r + 1) * count_x, m * LANES : (m + 1) * LANES]
            odd = result_ref[(2 * r + 1) * count_x : (2 * r + 2) * count_x, m * LANES : (m + 1) * LANES]
            if j % 2 == 0:
                value = jnp.where(low_half, even, pltpu.roll(odd, 64, 1))
            else:
                value = jnp.where(low_half, pltpu.roll(even, 64, 1), odd)
            out_ref[pl.ds(j * WIRE_ROWS + r, count_x, stride=stride), :] = value
        after = (j + 1) % count_y
        m = after // 2
        tail = jnp.where(lane == LANES - 1, mean, 0.0)
        for x in range(2 * PATCH_ROWS):
            value = result_ref[x * count_x : (x + 1) * count_x, m * LANES : (m + 1) * LANES]
            shift = (3 * x - 64 * (after % 2)) % LANES
            if shift:
                value = pltpu.roll(value, shift, 1)
            tail = jnp.where((lane >= 3 * x) & (lane < 3 * x + 3), value, tail)
        out_ref[pl.ds(j * WIRE_ROWS + PATCH_ROWS, count_x, stride=stride), :] = tail


def plane_call(wire, table, count_x, count_y):
    along_y = cas(np.arange(NY), wave_order(NY), NY)
    rows = 2 * PATCH_ROWS
    cell = (np.arange(rows)[:, None] + (NX // count_x) * np.arange(count_x)[None, :]).reshape(-1) % NX
    along_x = cas(cell, wave_order(NX), NX)
    square = np.concatenate([*high_low(along_y), *high_low(along_y.T), *high_low(along_x)], axis=0)
    wide = np.concatenate(high_low(along_x.T), axis=0)
    return pl.pallas_call(
        functools.partial(plane_kernel, count_x, count_y),
        out_shape=jax.ShapeDtypeStruct((PLANES * WIRE_ROWS, LANES), jnp.float32),
        scratch_shapes=[
            pltpu.VMEM((rows * count_x, NY), jnp.bfloat16),
            pltpu.VMEM((rows * count_x, NY), jnp.bfloat16),
            pltpu.VMEM((rows * count_x, NY), jnp.float32),
        ],
        compiler_params=pltpu.CompilerParams(vmem_limit_bytes=VMEM_BYTES),
        name="plane",
    )(wire, table, square, wide)


def force_kernel(
    wire_ref, place_ref, short_ref, charge_ref, basis_ref, energy_ref, force_ref, rows_ref
):
    for c in range(3):
        for bz in range(4):
            rows_ref[c, 4 * bz : 4 * bz + 4, :] = place_ref[c, bz, 1:5, :]
    pos_x, pos_y, pos_z = [row_vector(rows_ref[c]) for c in range(3)]
    planes = jnp.concatenate(
        [wire_ref[pl.ds(r, PLANES, stride=WIRE_ROWS), :] for r in range(WIRE_ROWS)], axis=1
    )
    basis = basis_ref[...]
    layers = dot3(split(basis), split(planes))
    mean = lax.dot_general(
        basis,
        planes[:, PATCH_ROWS * LANES :],
        NN,
        precision=lax.Precision.HIGHEST,
        preferred_element_type=jnp.float32,
    )[:, LANES - 1 :]
    high, low = split(layers)
    high, low = high.astype(jnp.float32), low.astype(jnp.float32)
    rest = jnp.zeros((LANES - 3 * ZPAD, layers.shape[1]), jnp.float32)
    columns = jnp.concatenate([high, high, low, rest], axis=0).T.astype(jnp.bfloat16)

    per = 4 * LANES
    for bx in range(4):
        cut = slice(bx * per, (bx + 1) * per)
        ux, uy = 8.0 * pos_x[:, cut], pos_y[:, cut]
        weight_z, slope_z = spline_both(z_distance(pos_z[:, cut]))
        z_both = jnp.concatenate([weight_z, slope_z], axis=1)
        z_high, z_low = split(z_both)
        z_high, z_low = z_high.astype(jnp.float32), z_low.astype(jnp.float32)
        z_rest = jnp.zeros((LANES - 3 * ZPAD, 2 * per), jnp.float32)
        z_table = jnp.concatenate([z_high, z_low, z_high, z_rest], axis=0).astype(jnp.bfloat16)
        weight_y, slope_y = spline_both(y_distance(uy, (64, per), iota((64, per), 0)))
        weight_x, slope_x = spline_both((iota((16, per), 0) - 1).astype(jnp.float32) - ux)
        def fold(value):
            out = value[0:8]
            for n in range(1, value.shape[0] // 8):
                out = out + value[8 * n : 8 * n + 8]
            return out

        zero = jnp.zeros((8, per), jnp.float32)
        total = [fold(weight_z * mean), zero, zero, fold(slope_z * mean)]
        for pair in range(6):
            r = 4 * bx + pair
            field = dot(columns[r * LANES : (r + 1) * LANES, :], z_table)
            for h in range(2):
                x = 2 * pair + h
                here = field[64 * h : 64 * h + 64, :per]
                slope = field[64 * h : 64 * h + 64, per:]
                plain = fold(here * weight_y)
                along_y = fold(here * slope_y)
                along_z = fold(slope * weight_y)
                wx, sx = weight_x[x : x + 1, :], slope_x[x : x + 1, :]
                total[0] = total[0] + plain * wx
                total[1] = total[1] + plain * sx
                total[2] = total[2] + along_y * wx
                total[3] = total[3] + along_z * wx
        field = dot(columns[PATCH_ROWS * LANES :, :], z_table)
        here, slope = field[:, :per], field[:, per:]
        place = iota((LANES, per), 0)
        tail_x, tail_sx = spline_both((place // 3 - 1 - 8 * bx).astype(jnp.float32) - ux)
        tail_y, tail_sy = spline_both(y_distance(uy, (LANES, per), 64 + place % 3))
        here_y = here * tail_y
        total[0] = total[0] + fold(here_y * tail_x)
        total[1] = total[1] + fold(here_y * tail_sx)
        total[2] = total[2] + fold(here * tail_sy * tail_x)
        total[3] = total[3] + fold(slope * tail_y * tail_x)
        sums = [jnp.sum(t, axis=0, keepdims=True) for t in total]
        for bz in range(4):
            at = slice(bz * LANES, (bz + 1) * LANES)
            charge = charge_ref[bz, bx : bx + 1, :]
            energy_ref[bz, bx : bx + 1, :] = short_ref[bz, bx : bx + 1, :] + 0.5 * charge * sums[0][:, at]
            for c in range(3):
                force_ref[c, bz, bx : bx + 1, :] = -charge * sums[1 + c][:, at]


def force_call(wire, place, short, charge):
    basis = np.zeros((ZPAD, PLANES))
    basis[:ZROWS] = cas(np.arange(ZROWS), np.arange(PLANES), PLANES)
    return pl.pallas_call(
        force_kernel,
        out_shape=(
            jax.ShapeDtypeStruct((4, 4, LANES), jnp.float32),
            jax.ShapeDtypeStruct((3, 4, 4, LANES), jnp.float32),
        ),
        scratch_shapes=[pltpu.VMEM((3, 16, LANES), jnp.float32)],
        compiler_params=pltpu.CompilerParams(vmem_limit_bytes=VMEM_BYTES),
        name="force",
    )(wire, place, short, charge, basis.astype(np.float32))


def ring(size):
    up = [(i, (i + 1) % size) for i in range(size)]
    return up, [(j, i) for i, j in up]


def exchange(wire):
    moved = lax.all_to_all(
        wire.reshape(PLANES, 1, WIRE_ROWS * LANES), ("gx", "gy"), split_axis=0, concat_axis=0, tiled=True
    )
    return moved.reshape(PLANES * WIRE_ROWS, LANES)


def shards(atom_cells, atom_frac, species, *weights):
    count_x, count_y = lax.axis_size("gx"), lax.axis_size("gy")
    assert count_x * count_y == PLANES and atom_cells.shape[1:] == (4, 4, LANES)
    place = ((atom_cells & (BLOCK - 1)).astype(jnp.float32) + atom_frac) * (1.0 / BLOCK)
    own = jnp.concatenate([place, species.astype(jnp.float32)[None]], axis=0)
    up, down = ring(count_x)
    before = lax.ppermute(own[:, :, 3:4, :], "gx", up)
    after = lax.ppermute(own[:, :, 0:1, :], "gx", down)
    ext = jnp.concatenate([before, own, after, after, after], axis=2)
    up, down = ring(count_y)
    left = lax.ppermute(ext, "gy", up)
    right = lax.ppermute(ext, "gy", down)
    table = filter_call(lax.axis_index(("gx", "gy")))
    packed = pack_weights(*weights)
    ext, left, right, packed, table = lax.optimization_barrier((ext, left, right, packed, table))
    short, charge, wire = atoms_call(ext, left, right, packed)
    wire = exchange(wire)
    wire = plane_call(wire, table, count_x, count_y)
    wire = exchange(wire)
    energy, force = force_call(wire, ext, short, charge)
    return energy, force, charge


def solution(mesh):
    atoms = P(None, "gx", "gy")
    vectors = P(None, None, "gx", "gy")
    return jax.shard_map(
        shards,
        mesh=mesh,
        in_specs=(vectors, vectors, atoms, P(), P(), P(), P(), P(), P()),
        out_specs=(atoms, vectors, atoms),
        check_vma=False,
    )
```

```python
import functools

import jax
import jax.numpy as jnp
import ml_dtypes
import numpy as np
from jax import lax
from jax.experimental import pallas as pl
from jax.experimental.pallas import tpu as pltpu
from jax.sharding import PartitionSpec as P

NX = 512
NY = 512
NZ = 256
BLOCK = 8
SLOTS = 16
ZBLOCKS = 4
RADIAL = 16
SPECIES = 2
NEURONS = 15
ZROWS = 35
ZPAD = 40
PLANES = 128
EWALD_BETA = 1.0
LANES = 128
PATCH_ROWS = 18
WIRE_ROWS = PATCH_ROWS + 1
NT = (((1,), (1,)), ((), ()))
NN = (((1,), (0,)), ((), ()))
TN = (((0,), (0,)), ((), ()))
VMEM_BYTES = 24 * 1024 * 1024


def high_low(table):
    high = table.astype(ml_dtypes.bfloat16)
    low = (table - high.astype(np.float64)).astype(ml_dtypes.bfloat16)
    return high, low


def split(value):
    high = value.astype(jnp.bfloat16)
    low = (value - high.astype(jnp.float32)).astype(jnp.bfloat16)
    return high, low


def dot(left, right, dims=NN):
    return lax.dot_general(left, right, dims, preferred_element_type=jnp.float32)


def dot3(left, right, dims=NN):
    return (
        dot(left[0], right[0], dims) + dot(left[0], right[1], dims) + dot(left[1], right[0], dims)
    )


def cas(left, right, length):
    angle = 2.0 * np.pi / length * (np.outer(left, right) % length)
    return np.cos(angle) + np.sin(angle)


def wave_order(length):
    half = length // 2
    return np.concatenate([np.arange(half + 1), length - np.arange(1, half)])


def axis_factor(wave, length):
    signed = np.where(wave > length // 2, wave - length, wave) / length
    smooth = 2.0 / 3.0 + np.cos(2.0 * np.pi / length * wave) / 3.0
    return signed**2, np.exp(-((np.pi / EWALD_BETA) ** 2) * signed**2) / smooth**2


def spline_weight(distance):
    away = jnp.abs(distance)
    outer = jnp.maximum(2.0 - away, 0.0)
    inner = jnp.maximum(1.0 - away, 0.0)
    return (outer * outer * outer - 4.0 * (inner * inner * inner)) * (1.0 / 6.0)


def spline_both(distance):
    away = jnp.abs(distance)
    outer = jnp.maximum(2.0 - away, 0.0)
    inner = jnp.maximum(1.0 - away, 0.0)
    outer_sq = outer * outer
    inner_sq = inner * inner
    weight = (outer_sq * outer - 4.0 * (inner_sq * inner)) * (1.0 / 6.0)
    slope = 0.5 * outer_sq - 2.0 * inner_sq
    return weight, jnp.where(distance > 0.0, slope, -slope)


def product_scale(k):
    return float(np.prod([f for n, f in enumerate((-2.0, 8.0, 128.0, 32768.0)) if k >> n & 1]))


def chebyshev_of_products(products):
    out = list(products)
    for top in (2, 4, 8):
        for first in range(0, RADIAL, 2 * top):
            for r in range(1, top):
                out[first + top + r] = 2.0 * out[first + top + r] - out[first + top - r]
    return out


def iota(shape, dim):
    return lax.broadcasted_iota(jnp.int32, shape, dim)


def row_vector(rows):
    return jnp.concatenate(
        [rows[bz * 4 + bx : bz * 4 + bx + 1, :] for bx in range(4) for bz in range(4)], axis=1
    )


def last_blocks(value):
    rows = value.shape[0]
    lane = iota((rows, LANES), 1)
    out = []
    for first in range(0, 16, 8):
        block = jnp.zeros((rows, LANES), value.dtype)
        for n in range(8):
            piece = value[:, (first + n) * LANES : (first + n + 1) * LANES]
            if n < 7:
                piece = pltpu.roll(piece, SLOTS * (n + 1), 1)
            block = jnp.where((lane >= SLOTS * n) & (lane < SLOTS * (n + 1)), piece, block)
        out.append(block)
    return jnp.concatenate(out, axis=1)


def tail_distances(pos_x, pos_y):
    shape = (LANES, pos_x.shape[1])
    place = iota(shape, 0)
    block = iota(shape, 1) // (ZBLOCKS * SLOTS)
    along_x = (place // 3 - 1 - 8 * block).astype(jnp.float32) - 8.0 * pos_x
    along_y = (64 - 1 - 8 * 7 + place % 3).astype(jnp.float32) - 8.0 * pos_y
    return along_x, along_y


def z_distance(pos_z):
    shape = (ZPAD, pos_z.shape[1])
    layer = (iota(shape, 1) // LANES) % ZBLOCKS
    return (iota(shape, 0) - 8 * layer - 1).astype(jnp.float32) - 8.0 * pos_z


def y_distance(pos_y, shape, cell):
    block = (iota(shape, 1) % LANES) // SLOTS
    return (cell - 1 - 8 * block).astype(jnp.float32) - 8.0 * pos_y


def place_blocks(near_ref, n, blocks, dx, dy):
    far = jnp.full((4, LANES), 100.0, jnp.float32)
    for c in range(4):
        offset = float((dx - 1, dy - 1, 0, 0)[c])
        for bz in range(ZBLOCKS):
            row = (c * ZBLOCKS + bz) * 8 + dx
            near_ref[n, c, 4 + 4 * bz : 8 + 4 * bz, :] = blocks[row : row + 4, :] + offset
        near_ref[n, c, 0:4, :] = far
        near_ref[n, c, 20:24, :] = far


def pair_sums(near_ref, count, center, mine, half, sums):
    lane8 = iota((8, LANES), 1)

    def body(n, sums):
        sums = list(sums)
        for dz in range(3):
            near = [near_ref[n, c, 4 * dz + 8 * half : 4 * dz + 8 * half + 8, :] for c in range(4)]
            mine_z = mine[2] - float(dz - 1)
            for turn in range(SLOTS):
                if turn == 0:
                    got = near
                else:
                    index = (lane8 & (LANES - SLOTS)) | ((lane8 + turn) & (SLOTS - 1))
                    got = [jnp.take_along_axis(v, index, axis=1) for v in near]
                gx = got[0] - mine[0]
                gy = got[1] - mine[1]
                gz = got[2] - mine_z
                kind = got[3]
                remain = jnp.maximum(1.0 - (gx * gx + gy * gy + gz * gz), 0.0)
                if turn == 0 and dz == 1 and center is not None:
                    remain = remain * jnp.where(n == center, 0.0, 1.0).astype(jnp.float32)
                half_t = remain - 0.5
                two = half_t * half_t - 1.0 / 8.0
                four = two * two - 1.0 / 128.0
                eight = four * four - 1.0 / 32768.0
                terms = [remain * remain]
                for factor in (half_t, two, four, eight):
                    terms = terms + [term * factor for term in terms]
                for k in range(RADIAL):
                    sums[k] = sums[k] + terms[k]
                    sums[RADIAL + k] = sums[RADIAL + k] + terms[k] * kind
        return tuple(sums)

    return lax.fori_loop(0, count, body, tuple(sums))


def first_pairs_kernel(ext_ref, sums_ref, near_ref):
    own = ext_ref[...].reshape(LANES, LANES)
    for dx in range(3):
        place_blocks(near_ref, dx, own, dx, 1)
    zero = jnp.zeros((8, LANES), jnp.float32)
    for half in range(2):
        at = slice(8 * half, 8 * half + 8)
        mine = [near_ref[1, c, 4 + 8 * half : 12 + 8 * half, :] for c in range(3)]
        sums = pair_sums(near_ref, 3, 1, mine, half, (zero,) * (2 * RADIAL))
        for k in range(2 * RADIAL):
            sums_ref[k, at, :] = sums[k]


def first_pairs_call(ext):
    return pl.pallas_call(
        first_pairs_kernel,
        out_shape=jax.ShapeDtypeStruct((SPECIES * RADIAL, 16, LANES), jnp.float32),
        scratch_shapes=[pltpu.VMEM((3, 4, 24, LANES), jnp.float32)],
        compiler_params=pltpu.CompilerParams(vmem_limit_bytes=VMEM_BYTES),
        cost_estimate=pl.CostEstimate(flops=24_000_000, bytes_accessed=1 << 19, transcendentals=0),
        name="first_pairs",
    )(ext)


def atoms_kernel(
    ext_ref,
    left_ref,
    right_ref,
    begun_ref,
    packed_ref,
    short_ref,
    charge_ref,
    wire_ref,
    near_ref,
    own_ref,
    feature_ref,
    weight_ref,
    bias_ref,
):
    lane = iota((LANES, LANES), 1)
    own = ext_ref[...].reshape(LANES, LANES)
    left = left_ref[...].reshape(LANES, LANES)
    right = right_ref[...].reshape(LANES, LANES)
    before = jnp.where(lane < SLOTS, pltpu.roll(left, SLOTS, 1), pltpu.roll(own, SLOTS, 1))
    after = jnp.where(
        lane >= LANES - SLOTS,
        pltpu.roll(right, LANES - SLOTS, 1),
        pltpu.roll(own, LANES - SLOTS, 1),
    )
    for dx in range(3):
        place_blocks(near_ref, 2 * dx, before, dx, 0)
        place_blocks(near_ref, 2 * dx + 1, after, dx, 2)
    for c in range(4):
        for bz in range(ZBLOCKS):
            row = (c * ZBLOCKS + bz) * 8 + 1
            own_ref[c, 4 * bz : 4 * bz + 4, :] = own[row : row + 4, :]

    for half in range(2):
        at = slice(8 * half, 8 * half + 8)
        mine = [own_ref[c, at, :] for c in range(3)]
        begun = [begun_ref[k, at, :] for k in range(2 * RADIAL)]
        sums = pair_sums(near_ref, 6, None, mine, half, begun)
        scales = [product_scale(k) / SLOTS for k in range(RADIAL)]
        both = chebyshev_of_products([sums[k] * scales[k] for k in range(RADIAL)])
        ones = chebyshev_of_products([sums[RADIAL + k] * scales[k] for k in range(RADIAL)])
        for k in range(RADIAL):
            feature_ref[k, 8 * half : 8 * half + 8, :] = both[k] - ones[k]
            feature_ref[RADIAL + k, 8 * half : 8 * half + 8, :] = ones[k]

    features = jnp.concatenate(
        [feature_ref[:, bz * 4 + bx, :] for bx in range(4) for bz in range(4)], axis=1
    )
    weight_ref[...] = jnp.zeros(weight_ref.shape, jnp.float32)
    bias_ref[...] = jnp.zeros(bias_ref.shape, jnp.float32)
    for s in range(SPECIES):
        at = s * 16
        weight_ref[0, at : at + NEURONS, : SPECIES * RADIAL] = packed_ref[:15, s, : SPECIES * RADIAL]
        weight_ref[1, at : at + NEURONS, at : at + NEURONS] = packed_ref[15:30, s, :NEURONS]
        weight_ref[2, 2 * s : 2 * s + 2, at : at + NEURONS] = packed_ref[30 + s, :, :NEURONS]
        bias_ref[0:1, at : at + NEURONS] = packed_ref[32, s : s + 1, :NEURONS]
        bias_ref[1:2, at : at + NEURONS] = packed_ref[33, s : s + 1, :NEURONS]
        bias_ref[2:3, 2 * s : 2 * s + 2] = packed_ref[34, s : s + 1, :2]
    diagonal = iota((LANES, LANES), 0) == iota((LANES, LANES), 1)

    def layer(n, x, height):
        bias = jnp.sum(
            jnp.where(diagonal[:height], bias_ref[n : n + 1, :], 0.0), axis=1, keepdims=True
        )
        full = lax.dot_general(
            weight_ref[n, :height, :32], x, TN if n == 1 else NN, precision=lax.Precision.HIGHEST, preferred_element_type=jnp.float32
        )
        return full + bias

    rows = [own_ref[c] for c in range(4)]
    pos_x, pos_y, pos_z, kinds = [row_vector(r) for r in rows]
    answers = layer(2, jnp.tanh(layer(1, jnp.tanh(layer(0, features, 32)), 32)), 8)
    answer = jnp.where(kinds == 0.0, answers[0:2, :], answers[2:4, :])
    charge = answer[1:2, :]
    for bx in range(4):
        for bz in range(4):
            at = (bx * 4 + bz) * LANES
            short_ref[bz, bx : bx + 1, :] = answer[0:1, at : at + LANES]
            charge_ref[bz, bx : bx + 1, :] = charge[:, at : at + LANES]

    along_z = split(spline_weight(z_distance(pos_z)))
    basis = jnp.concatenate([packed_ref[35:, n, :ZPAD] for n in range(2)], axis=0)
    waves = dot3(split(basis), along_z) * charge
    waves_high, waves_low = split(waves)

    per = 4 * LANES
    carry = [None, None]
    for bx in range(4):
        cut = slice(bx * per, (bx + 1) * per)
        ux, uy = 8.0 * pos_x[:, cut], pos_y[:, cut]
        waves_cut = (waves_high[:, cut], waves_low[:, cut])
        weight_y = spline_weight(y_distance(uy, (64, per), iota((64, per), 0)))
        weight_x = spline_weight((iota((16, per), 0) - 1).astype(jnp.float32) - ux)
        for group in range(3):
            product = jnp.concatenate(
                [weight_y * weight_x[4 * group + h : 4 * group + h + 1, :] for h in range(4)], axis=0
            )
            both = dot3(waves_cut, split(product), NT)
            for n in range(2):
                pair = 2 * group + n
                plane = both[:, n * LANES : (n + 1) * LANES]
                if pair < 2 and bx > 0:
                    plane = plane + carry[pair]
                if pair >= 4 and bx < 3:
                    carry[pair - 4] = plane
                else:
                    wire_ref[pl.ds(4 * bx + pair, PLANES, stride=WIRE_ROWS), :] = plane
    tail_x, tail_y = tail_distances(last_blocks(pos_x), last_blocks(pos_y))
    product = spline_weight(tail_x) * spline_weight(tail_y)
    tail = dot3(split(last_blocks(waves)), split(product), NT)
    wire_ref[pl.ds(PATCH_ROWS, PLANES, stride=WIRE_ROWS), :] = tail


def pack_weights(w_first, b_first, w_second, b_second, w_out, b_out):
    parts = [
        w_first.transpose(2, 0, 1),
        w_second.transpose(1, 0, 2),
        w_out.transpose(0, 2, 1),
        b_first[None],
        b_second[None],
        b_out[None],
    ]
    basis = np.zeros((2, PLANES // 2, LANES), np.float32)
    basis[:, :, :ZROWS] = cas(np.arange(PLANES), np.arange(ZROWS), PLANES).reshape(2, PLANES // 2, ZROWS)
    parts.append(basis.transpose(1, 0, 2))
    height = sum(part.shape[0] for part in parts)
    total, first = 0.0, 0
    for part in parts:
        after = height - first - part.shape[0]
        total = total + jnp.pad(part, ((first, after), (0, 0), (0, LANES - part.shape[2])))
        first += part.shape[0]
    return total


def atoms_call(ext, left, right, begun, packed):
    f32 = jnp.float32
    return pl.pallas_call(
        atoms_kernel,
        out_shape=(
            jax.ShapeDtypeStruct((4, 4, LANES), f32),
            jax.ShapeDtypeStruct((4, 4, LANES), f32),
            jax.ShapeDtypeStruct((PLANES * WIRE_ROWS, LANES), f32),
        ),
        scratch_shapes=[
            pltpu.VMEM((6, 4, 24, LANES), f32),
            pltpu.VMEM((4, 16, LANES), f32),
            pltpu.VMEM((SPECIES * RADIAL, 16, LANES), f32),
            pltpu.VMEM((3, 32, LANES), f32),
            pltpu.VMEM((8, LANES), f32),
        ],
        compiler_params=pltpu.CompilerParams(vmem_limit_bytes=VMEM_BYTES),
        name="atoms",
    )(ext, left, right, begun, packed)


def filter_kernel(terms_ref, squares_ref, row_ref, column_ref, out_ref):
    half = NX // 2
    count = NZ // 4

    def series(square):
        total = None
        for t in range(1, count + 1, 4):
            near = [square + squares_ref[t + n] for n in range(4)]
            parts = [
                (
                    terms_ref[t + n] * near[n + 1] + terms_ref[t + n + 1] * near[n],
                    near[n] * near[n + 1],
                )
                for n in (0, 2)
            ]
            part = (parts[0][0] * parts[1][1] + parts[1][0] * parts[0][1]) / (
                parts[0][1] * parts[1][1]
            )
            total = part if total is None else total + part
        even = square + squares_ref[0]
        extra = terms_ref[0] / jnp.where(even > 0.0, even, 1.0)
        return total + jnp.where(even > 0.0, extra, 0.0)

    edge = series(row_ref[0:8, :] + 0.25) * row_ref[8:16, :] * column_ref[half : half + 8, 1:2]
    edge = edge[0:1, :]
    edge_low, edge_corner = edge[:, :half], edge[:, half : half + 1]
    first_lane = iota((16, half), 1) == 0

    def body(n, _):
        at = pl.multiple_of(n * 16, 16)
        column = column_ref[pl.ds(at, 16), :]
        value = series(row_ref[0:1, :half] + column[:, 0:1]) * row_ref[8:9, :half] * column[:, 1:2]
        row = at + iota((16, half), 0)
        mirror = jnp.sum(
            jnp.where(row == iota((16, half), 1), edge_low, 0.0), axis=1, keepdims=True
        )
        right = jnp.where(first_lane, mirror, value)
        out_ref[pl.ds(at, 16), :half] = value
        out_ref[pl.ds(at, 16), half:] = right
        out_ref[pl.ds(half + at, 16), :half] = jnp.where(row == 0, edge_low, value)
        corner = jnp.where(first_lane, edge_corner, edge_low)
        out_ref[pl.ds(half + at, 16), half:] = jnp.where(row == 0, corner, right)
        return 0

    lax.fori_loop(0, half // 16, body, 0)


def filter_tables():
    plane = np.arange(PLANES)[:, None]
    odd = np.arange(1, NZ // 2, 2)
    gaps = np.arange(-(PLANES // 2) + 1, PLANES // 2 + 1)
    window = np.cos(2.0 * np.pi / PLANES * plane * gaps) @ np.cos(
        2.0 * np.pi / NZ * gaps[:, None] * odd
    )
    even = 2 * np.minimum(plane, PLANES - plane)
    wave = np.concatenate([even, np.broadcast_to(odd, (PLANES, odd.size))], axis=1)
    square, factor = axis_factor(wave, NZ)
    count = np.concatenate([np.full((PLANES, 1), float(PLANES)), 2.0 * window], axis=1)
    terms = count * factor / (np.pi * NX * NY * NZ * PLANES)
    return terms.astype(np.float32), square.astype(np.float32)


def filter_call(plane):
    terms, squares = filter_tables()
    square, factor = axis_factor(wave_order(NX), NX)
    row = np.repeat(np.stack([square, factor]), 8, axis=0).astype(np.float32)
    column = np.stack([square, factor], axis=1).astype(np.float32)
    smem = pl.BlockSpec(memory_space=pltpu.SMEM)
    vmem = pl.BlockSpec(memory_space=pltpu.VMEM)
    return pl.pallas_call(
        filter_kernel,
        out_shape=jax.ShapeDtypeStruct((NX, NY), jnp.float32),
        in_specs=[smem, smem, vmem, vmem],
        compiler_params=pltpu.CompilerParams(vmem_limit_bytes=VMEM_BYTES),
        cost_estimate=pl.CostEstimate(flops=20_000_000, bytes_accessed=1 << 20, transcendentals=0),
        name="filter",
    )(
        lax.dynamic_index_in_dim(jnp.asarray(terms), plane, 0, keepdims=False),
        lax.dynamic_index_in_dim(jnp.asarray(squares), plane, 0, keepdims=False),
        row,
        column,
    )


def plane_kernel(
    count_x,
    count_y,
    wire_ref,
    filter_ref,
    table_ref,
    out_ref,
    grid_high,
    grid_low,
    result_ref,
    y_high,
    y_low,
    yt_high,
    yt_low,
    x_high,
    x_low,
    xt_high,
    xt_low,
):
    width = x_high.shape[0]

    def fill(high_ref, low_ref, first, value):
        high_ref[first : first + 16, :], low_ref[first : first + 16, :] = split(value)

    def part(name, lanes):
        first, height = TABLE[name]
        return table_ref[first : first + height, :lanes]

    cosine, sine = part("y cos", NY), part("y sin", NY)
    for a in range(32):
        at = slice(a, a + 1)
        fill(y_high, y_low, 16 * a, cosine[at] * part("y cas", NY) + sine[at] * part("y sac", NY))
    cosine, sine = part("x cos", NX), part("x sin", NX)
    plus, minus = part("x cas", NX), part("x sac", NX)
    for x in range(2 * PATCH_ROWS):
        at = slice(x, x + 1)
        fill(x_high, x_low, 16 * x, cosine * plus[at] + sine * minus[at])
    for name, lanes, high, low in (("yt", NY, yt_high, yt_low), ("xt", width, xt_high, xt_low)):
        cosine, sine = part(name + " cos", lanes), part(name + " sin", lanes)
        plus, minus = part(name + " cas", lanes), part(name + " sac", lanes)
        middle = part(name + " mid", lanes)[0:1]
        for a in range(16):
            at = slice(a, a + 1)
            fill(high, low, 16 * a, cosine[at] * plus + sine[at] * minus)
            value = cosine[at] * minus - sine[at] * plus
            if a == 0:
                value = jnp.where(iota((16, lanes), 0) == 0, middle, value)
            fill(high, low, 256 + 16 * a, value)

    stride = count_y * WIRE_ROWS
    pairs = count_y // 2
    lane = iota((count_x, LANES), 1)
    low_half = lane < 64
    tails = [wire_ref[pl.ds(j * WIRE_ROWS + PATCH_ROWS, count_x, stride=stride), :] for j in range(count_y)]
    for m in range(pairs):
        before = tails[(2 * m - 1) % count_y]
        between = tails[2 * m]
        for r in range(PATCH_ROWS):
            one = wire_ref[pl.ds(2 * m * WIRE_ROWS + r, count_x, stride=stride), :]
            two = wire_ref[pl.ds((2 * m + 1) * WIRE_ROWS + r, count_x, stride=stride), :]
            for h in range(2):
                x = 2 * r + h
                if h == 0:
                    value = jnp.where(low_half, one, pltpu.roll(two, 64, 1))
                else:
                    value = jnp.where(low_half, pltpu.roll(one, 64, 1), two)
                first = pltpu.roll(before, (LANES - 3 * x) % LANES, 1) if x else before
                second = pltpu.roll(between, (LANES + 64 - 3 * x) % LANES, 1)
                value = value + jnp.where(lane < 3, first, 0.0)
                value = value + jnp.where((lane >= 64) & (lane < 67), second, 0.0)
                high, low = split(value)
                at = x * count_x
                grid_high[at : at + count_x, m * LANES : (m + 1) * LANES] = high
                grid_low[at : at + count_x, m * LANES : (m + 1) * LANES] = low

    step = split(dot3((grid_high[...], grid_low[...]), (y_high[...], y_low[...])))
    spectrum = dot3((xt_high[...], xt_low[...]), step) * filter_ref[...]
    mean = spectrum[0:1, 0:1]
    first = (iota((8, NX), 0) == 0) & (iota((8, NX), 1) == 0)
    spectrum = jnp.concatenate([jnp.where(first, 0.0, spectrum[:8]), spectrum[8:]], axis=0)
    step = split(dot3((x_high[...], x_low[...]), split(spectrum)))
    result_ref[...] = dot3(step, (yt_high[...], yt_low[...]))

    for j in range(count_y):
        m = j // 2
        for r in range(PATCH_ROWS):
            even = result_ref[2 * r * count_x : (2 * r + 1) * count_x, m * LANES : (m + 1) * LANES]
            odd = result_ref[(2 * r + 1) * count_x : (2 * r + 2) * count_x, m * LANES : (m + 1) * LANES]
            if j % 2 == 0:
                value = jnp.where(low_half, even, pltpu.roll(odd, 64, 1))
            else:
                value = jnp.where(low_half, pltpu.roll(even, 64, 1), odd)
            out_ref[pl.ds(j * WIRE_ROWS + r, count_x, stride=stride), :] = value
        after = (j + 1) % count_y
        m = after // 2
        tail = jnp.where(lane == LANES - 1, mean, 0.0)
        for x in range(2 * PATCH_ROWS):
            value = result_ref[x * count_x : (x + 1) * count_x, m * LANES : (m + 1) * LANES]
            shift = (3 * x - 64 * (after % 2)) % LANES
            if shift:
                value = pltpu.roll(value, shift, 1)
            tail = jnp.where((lane >= 3 * x) & (lane < 3 * x + 3), value, tail)
        out_ref[pl.ds(j * WIRE_ROWS + PATCH_ROWS, count_x, stride=stride), :] = tail


def table_layout():
    heights = {"y cos": 32, "y sin": 32, "y cas": 16, "y sac": 16}
    heights.update({"x cos": 16, "x sin": 16, "x cas": 40, "x sac": 40})
    for name in ("yt", "xt"):
        heights.update({name + " cos": 16, name + " sin": 16, name + " cas": 16, name + " sac": 16, name + " mid": 8})
    layout, first = {}, 0
    for name, height in heights.items():
        layout[name] = (first, height)
        first += height
    return layout, first


TABLE, TABLE_ROWS = table_layout()


def plane_tables(count_x):
    wave, cell = wave_order(NY), np.arange(NY)
    place = (np.arange(2 * PATCH_ROWS)[:, None] + (NX // count_x) * np.arange(count_x)).reshape(-1)
    out = np.zeros((TABLE_ROWS, 640), np.float32)

    def put(name, rows, lanes):
        angle = 2.0 * np.pi / NX * (np.outer(rows, lanes) % NX)
        cosine, sine = np.cos(angle), np.sin(angle)
        value = {"cos": cosine, "sin": sine, "cas": cosine + sine, "sac": cosine - sine, "mid": cosine}
        first = TABLE[name][0]
        out[first : first + len(rows), : len(lanes)] = value[name[-3:]]

    sixteen = np.arange(16)
    for kind in ("cos", "sin"):
        put("y " + kind, 16 * np.arange(32), wave)
        put("x " + kind, (NX // count_x) * np.arange(count_x), wave)
        put("yt " + kind, 16 * sixteen, cell)
        put("xt " + kind, 16 * sixteen, place)
    for kind in ("cas", "sac"):
        put("y " + kind, sixteen, wave)
        put("x " + kind, np.arange(2 * PATCH_ROWS), wave)
        put("yt " + kind, sixteen, cell)
        put("xt " + kind, sixteen, place)
    put("yt mid", np.array([NY // 2]), cell)
    put("xt mid", np.array([NX // 2]), place)
    return out


def plane_call(wire, table, tables, count_x, count_y):
    rows = 2 * PATCH_ROWS
    return pl.pallas_call(
        functools.partial(plane_kernel, count_x, count_y),
        out_shape=jax.ShapeDtypeStruct((PLANES * WIRE_ROWS, LANES), jnp.float32),
        scratch_shapes=[
            pltpu.VMEM((rows * count_x, NY), jnp.bfloat16),
            pltpu.VMEM((rows * count_x, NY), jnp.bfloat16),
            pltpu.VMEM((rows * count_x, NY), jnp.float32),
            *[pltpu.VMEM((NY, NY), jnp.bfloat16)] * 4,
            *[pltpu.VMEM((rows * count_x, NX), jnp.bfloat16)] * 2,
            *[pltpu.VMEM((NX, rows * count_x), jnp.bfloat16)] * 2,
        ],
        compiler_params=pltpu.CompilerParams(vmem_limit_bytes=VMEM_BYTES),
        name="plane",
    )(wire, table, tables)


def force_kernel(
    wire_ref, place_ref, short_ref, charge_ref, basis_ref, energy_ref, force_ref, rows_ref
):
    for c in range(3):
        for bz in range(4):
            rows_ref[c, 4 * bz : 4 * bz + 4, :] = place_ref[c, bz, 1:5, :]
    pos_x, pos_y, pos_z = [row_vector(rows_ref[c]) for c in range(3)]
    planes = jnp.concatenate(
        [wire_ref[pl.ds(r, PLANES, stride=WIRE_ROWS), :] for r in range(WIRE_ROWS)], axis=1
    )
    basis = basis_ref[...]
    layers = dot3(split(basis), split(planes))
    mean = lax.dot_general(
        basis,
        planes[:, PATCH_ROWS * LANES :],
        NN,
        precision=lax.Precision.HIGHEST,
        preferred_element_type=jnp.float32,
    )[:, LANES - 1 :]
    high, low = split(layers)
    high, low = high.astype(jnp.float32), low.astype(jnp.float32)
    rest = jnp.zeros((LANES - 3 * ZPAD, layers.shape[1]), jnp.float32)
    columns = jnp.concatenate([high, high, low, rest], axis=0).T.astype(jnp.bfloat16)

    def fold(value):
        out = value[0:8]
        for n in range(1, value.shape[0] // 8):
            out = out + value[8 * n : 8 * n + 8]
        return out

    def z_table(weight, slope):
        high, low = split(jnp.concatenate([weight, slope], axis=1))
        high, low = high.astype(jnp.float32), low.astype(jnp.float32)
        rest = jnp.zeros((LANES - 3 * ZPAD, high.shape[1]), jnp.float32)
        return jnp.concatenate([high, low, high, rest], axis=0).astype(jnp.bfloat16)

    last_x, last_y, last_z = [last_blocks(v) for v in (pos_x, pos_y, pos_z)]
    size = last_x.shape[1]
    layer = (iota((ZPAD, size), 1) // SLOTS) % ZBLOCKS
    last_distance = (iota((ZPAD, size), 0) - 8 * layer - 1).astype(jnp.float32) - 8.0 * last_z
    field = dot(columns[PATCH_ROWS * LANES :, :], z_table(*spline_both(last_distance)))
    here, slope = field[:, :size], field[:, size:]
    tail_x, tail_y = tail_distances(last_x, last_y)
    (tail_x, tail_sx), (tail_y, tail_sy) = spline_both(tail_x), spline_both(tail_y)
    here_y = here * tail_y
    tails = [
        jnp.sum(fold(v), axis=0, keepdims=True)
        for v in (here_y * tail_x, here_y * tail_sx, here * tail_sy * tail_x, slope * tail_y * tail_x)
    ]
    last_lanes = iota((1, LANES), 1) >= LANES - SLOTS

    def tail_of(n, bx, bz):
        at = bx * ZBLOCKS + bz
        half = tails[n][:, (at // 8) * LANES : (at // 8 + 1) * LANES]
        shift = (LANES - SLOTS * (at % 8 + 1)) % LANES
        return jnp.where(last_lanes, pltpu.roll(half, shift, 1) if shift else half, 0.0)

    per = 4 * LANES
    for bx in range(4):
        cut = slice(bx * per, (bx + 1) * per)
        ux, uy = 8.0 * pos_x[:, cut], pos_y[:, cut]
        weight_z, slope_z = spline_both(z_distance(pos_z[:, cut]))
        table = z_table(weight_z, slope_z)
        weight_y, slope_y = spline_both(y_distance(uy, (64, per), iota((64, per), 0)))
        weight_x, slope_x = spline_both((iota((16, per), 0) - 1).astype(jnp.float32) - ux)
        zero = jnp.zeros((8, per), jnp.float32)
        total = [fold(weight_z * mean), zero, zero, fold(slope_z * mean)]
        for pair in range(6):
            r = 4 * bx + pair
            field = dot(columns[r * LANES : (r + 1) * LANES, :], table)
            for h in range(2):
                x = 2 * pair + h
                here = field[64 * h : 64 * h + 64, :per]
                slope = field[64 * h : 64 * h + 64, per:]
                plain = fold(here * weight_y)
                along_y = fold(here * slope_y)
                along_z = fold(slope * weight_y)
                wx, sx = weight_x[x : x + 1, :], slope_x[x : x + 1, :]
                total[0] = total[0] + plain * wx
                total[1] = total[1] + plain * sx
                total[2] = total[2] + along_y * wx
                total[3] = total[3] + along_z * wx
        sums = [jnp.sum(t, axis=0, keepdims=True) for t in total]
        for bz in range(4):
            at = slice(bz * LANES, (bz + 1) * LANES)
            charge = charge_ref[bz, bx : bx + 1, :]
            found = [sums[n][:, at] + tail_of(n, bx, bz) for n in range(4)]
            energy_ref[bz, bx : bx + 1, :] = short_ref[bz, bx : bx + 1, :] + 0.5 * charge * found[0]
            for c in range(3):
                force_ref[c, bz, bx : bx + 1, :] = -charge * found[1 + c]


def force_call(wire, place, short, charge):
    basis = np.zeros((ZPAD, PLANES))
    basis[:ZROWS] = cas(np.arange(ZROWS), np.arange(PLANES), PLANES)
    return pl.pallas_call(
        force_kernel,
        out_shape=(
            jax.ShapeDtypeStruct((4, 4, LANES), jnp.float32),
            jax.ShapeDtypeStruct((3, 4, 4, LANES), jnp.float32),
        ),
        scratch_shapes=[pltpu.VMEM((3, 16, LANES), jnp.float32)],
        compiler_params=pltpu.CompilerParams(vmem_limit_bytes=VMEM_BYTES),
        name="force",
    )(wire, place, short, charge, basis.astype(np.float32))


def ring(size):
    up = [(i, (i + 1) % size) for i in range(size)]
    return up, [(j, i) for i, j in up]


def exchange(wire):
    moved = lax.all_to_all(
        wire.reshape(PLANES, 1, WIRE_ROWS * LANES), ("gx", "gy"), split_axis=0, concat_axis=0, tiled=True
    )
    return moved.reshape(PLANES * WIRE_ROWS, LANES)


def shards(atom_cells, atom_frac, species, *weights):
    count_x, count_y = lax.axis_size("gx"), lax.axis_size("gy")
    assert count_x * count_y == PLANES and atom_cells.shape[1:] == (4, 4, LANES)
    place = ((atom_cells & (BLOCK - 1)).astype(jnp.float32) + atom_frac) * (1.0 / BLOCK)
    kinds = species.astype(jnp.float32)[None]
    own = jnp.pad(place, ((0, 1), (0, 0), (0, 0), (0, 0)))
    own = jnp.where(lax.broadcasted_iota(jnp.int32, own.shape, 0) == 3, kinds, own)
    up, down = ring(count_x)
    before = lax.ppermute(own[:, :, 3:4, :], "gx", up)
    after = lax.ppermute(own[:, :, 0:1, :], "gx", down)
    ext = jnp.concatenate([before, own, after, after, after], axis=2)
    up, down = ring(count_y)
    left = lax.ppermute(ext, "gy", up)
    right = lax.ppermute(ext, "gy", down)
    tables = plane_tables(count_x)
    table = filter_call(lax.axis_index(("gx", "gy")))
    begun = first_pairs_call(ext)
    short, charge, wire = atoms_call(ext, left, right, begun, pack_weights(*weights))
    wire = exchange(wire)
    wire = plane_call(wire, table, tables, count_x, count_y)
    wire = exchange(wire)
    energy, force = force_call(wire, ext, short, charge)
    return energy, force, charge


def solution(mesh):
    atoms = P(None, "gx", "gy")
    vectors = P(None, None, "gx", "gy")
    return jax.shard_map(
        shards,
        mesh=mesh,
        in_specs=(vectors, vectors, atoms, P(), P(), P(), P(), P(), P()),
        out_specs=(atoms, vectors, atoms),
        check_vma=False,
    )
```

```python
import functools

import jax
import jax.numpy as jnp
import ml_dtypes
import numpy as np
from jax import lax
from jax.experimental import pallas as pl
from jax.experimental.pallas import tpu as pltpu
from jax.sharding import PartitionSpec as P

NX = 512
NY = 512
NZ = 256
BLOCK = 8
SLOTS = 16
ZBLOCKS = 4
RADIAL = 16
SPECIES = 2
NEURONS = 15
ZROWS = 35
ZPAD = 40
PLANES = 128
EWALD_BETA = 1.0
LANES = 128
PATCH_ROWS = 18
WIRE_ROWS = PATCH_ROWS + 1
NT = (((1,), (1,)), ((), ()))
NN = (((1,), (0,)), ((), ()))
TN = (((0,), (0,)), ((), ()))
VMEM_BYTES = 24 * 1024 * 1024


def high_low(table):
    high = table.astype(ml_dtypes.bfloat16)
    low = (table - high.astype(np.float64)).astype(ml_dtypes.bfloat16)
    return high, low


def split(value):
    high = value.astype(jnp.bfloat16)
    low = (value - high.astype(jnp.float32)).astype(jnp.bfloat16)
    return high, low


def dot(left, right, dims=NN):
    return lax.dot_general(left, right, dims, preferred_element_type=jnp.float32)


def dot3(left, right, dims=NN):
    return (
        dot(left[0], right[0], dims) + dot(left[0], right[1], dims) + dot(left[1], right[0], dims)
    )


def cas(left, right, length):
    angle = 2.0 * np.pi / length * (np.outer(left, right) % length)
    return np.cos(angle) + np.sin(angle)


def wave_order(length):
    half = length // 2
    return np.concatenate([np.arange(half + 1), length - np.arange(1, half)])


def axis_factor(wave, length):
    signed = np.where(wave > length // 2, wave - length, wave) / length
    smooth = 2.0 / 3.0 + np.cos(2.0 * np.pi / length * wave) / 3.0
    return signed**2, np.exp(-((np.pi / EWALD_BETA) ** 2) * signed**2) / smooth**2


def spline_weight(distance):
    away = jnp.abs(distance)
    outer = jnp.maximum(2.0 - away, 0.0)
    inner = jnp.maximum(1.0 - away, 0.0)
    return (outer * outer * outer - 4.0 * (inner * inner * inner)) * (1.0 / 6.0)


def spline_both(distance):
    away = jnp.abs(distance)
    outer = jnp.maximum(2.0 - away, 0.0)
    inner = jnp.maximum(1.0 - away, 0.0)
    outer_sq = outer * outer
    inner_sq = inner * inner
    weight = (outer_sq * outer - 4.0 * (inner_sq * inner)) * (1.0 / 6.0)
    slope = 0.5 * outer_sq - 2.0 * inner_sq
    return weight, jnp.where(distance > 0.0, slope, -slope)


def product_scale(k):
    return float(np.prod([f for n, f in enumerate((-2.0, 8.0, 128.0, 32768.0)) if k >> n & 1]))


def chebyshev_of_products(products):
    out = list(products)
    for top in (2, 4, 8):
        for first in range(0, RADIAL, 2 * top):
            for r in range(1, top):
                out[first + top + r] = 2.0 * out[first + top + r] - out[first + top - r]
    return out


def iota(shape, dim):
    return lax.broadcasted_iota(jnp.int32, shape, dim)


def row_vector(rows):
    return jnp.concatenate(
        [rows[bz * 4 + bx : bz * 4 + bx + 1, :] for bx in range(4) for bz in range(4)], axis=1
    )


def last_blocks(value):
    rows = value.shape[0]
    lane = iota((rows, LANES), 1)
    out = []
    for first in range(0, 16, 8):
        block = jnp.zeros((rows, LANES), value.dtype)
        for n in range(8):
            piece = value[:, (first + n) * LANES : (first + n + 1) * LANES]
            if n < 7:
                piece = pltpu.roll(piece, SLOTS * (n + 1), 1)
            block = jnp.where((lane >= SLOTS * n) & (lane < SLOTS * (n + 1)), piece, block)
        out.append(block)
    return jnp.concatenate(out, axis=1)


def tail_distances(pos_x, pos_y):
    shape = (LANES, pos_x.shape[1])
    place = iota(shape, 0)
    block = iota(shape, 1) // (ZBLOCKS * SLOTS)
    along_x = (place // 3 - 1 - 8 * block).astype(jnp.float32) - 8.0 * pos_x
    along_y = (64 - 1 - 8 * 7 + place % 3).astype(jnp.float32) - 8.0 * pos_y
    return along_x, along_y


def z_distance(pos_z):
    shape = (ZPAD, pos_z.shape[1])
    layer = (iota(shape, 1) // LANES) % ZBLOCKS
    return (iota(shape, 0) - 8 * layer - 1).astype(jnp.float32) - 8.0 * pos_z


def y_distance(pos_y, shape, cell):
    block = (iota(shape, 1) % LANES) // SLOTS
    return (cell - 1 - 8 * block).astype(jnp.float32) - 8.0 * pos_y


def place_blocks(near_ref, n, blocks, dx, dy):
    far = jnp.full((4, LANES), 100.0, jnp.float32)
    for c in range(4):
        offset = float((dx - 1, dy - 1, 0, 0)[c])
        for bz in range(ZBLOCKS):
            row = (c * ZBLOCKS + bz) * 8 + dx
            near_ref[n, c, 4 + 4 * bz : 8 + 4 * bz, :] = blocks[row : row + 4, :] + offset
        near_ref[n, c, 0:4, :] = far
        near_ref[n, c, 20:24, :] = far


def pair_sums(near_ref, count, center, mine, half, sums):
    lane8 = iota((8, LANES), 1)

    def body(n, sums):
        sums = list(sums)
        for dz in range(3):
            near = [near_ref[n, c, 4 * dz + 8 * half : 4 * dz + 8 * half + 8, :] for c in range(4)]
            mine_z = mine[2] - float(dz - 1)
            for turn in range(SLOTS):
                if turn == 0:
                    got = near
                else:
                    index = (lane8 & (LANES - SLOTS)) | ((lane8 + turn) & (SLOTS - 1))
                    got = [jnp.take_along_axis(v, index, axis=1) for v in near]
                gx = got[0] - mine[0]
                gy = got[1] - mine[1]
                gz = got[2] - mine_z
                kind = got[3]
                remain = jnp.maximum(1.0 - (gx * gx + gy * gy + gz * gz), 0.0)
                if turn == 0 and dz == 1 and center is not None:
                    remain = remain * jnp.where(n == center, 0.0, 1.0).astype(jnp.float32)
                half_t = remain - 0.5
                two = half_t * half_t - 1.0 / 8.0
                four = two * two - 1.0 / 128.0
                eight = four * four - 1.0 / 32768.0
                terms = [remain * remain]
                for factor in (half_t, two, four, eight):
                    terms = terms + [term * factor for term in terms]
                for k in range(RADIAL):
                    sums[k] = sums[k] + terms[k]
                    sums[RADIAL + k] = sums[RADIAL + k] + terms[k] * kind
        return tuple(sums)

    return lax.fori_loop(0, count, body, tuple(sums))


def first_pairs_kernel(ext_ref, sums_ref, near_ref):
    own = ext_ref[...].reshape(LANES, LANES)
    for dx in range(3):
        place_blocks(near_ref, dx, own, dx, 1)
    zero = jnp.zeros((8, LANES), jnp.float32)
    for half in range(2):
        at = slice(8 * half, 8 * half + 8)
        mine = [near_ref[1, c, 4 + 8 * half : 12 + 8 * half, :] for c in range(3)]
        sums = pair_sums(near_ref, 3, 1, mine, half, (zero,) * (2 * RADIAL))
        for k in range(2 * RADIAL):
            sums_ref[k, at, :] = sums[k]


def first_pairs_call(ext):
    return pl.pallas_call(
        first_pairs_kernel,
        out_shape=jax.ShapeDtypeStruct((SPECIES * RADIAL, 16, LANES), jnp.float32),
        scratch_shapes=[pltpu.VMEM((3, 4, 24, LANES), jnp.float32)],
        compiler_params=pltpu.CompilerParams(vmem_limit_bytes=VMEM_BYTES),
        cost_estimate=pl.CostEstimate(flops=24_000_000, bytes_accessed=1 << 19, transcendentals=0),
        name="first_pairs",
    )(ext)


def atoms_kernel(
    ext_ref,
    left_ref,
    right_ref,
    begun_ref,
    packed_ref,
    short_ref,
    charge_ref,
    wire_ref,
    near_ref,
    own_ref,
    feature_ref,
    weight_ref,
    bias_ref,
):
    lane = iota((LANES, LANES), 1)
    own = ext_ref[...].reshape(LANES, LANES)
    left = left_ref[...].reshape(LANES, LANES)
    right = right_ref[...].reshape(LANES, LANES)
    before = jnp.where(lane < SLOTS, pltpu.roll(left, SLOTS, 1), pltpu.roll(own, SLOTS, 1))
    after = jnp.where(
        lane >= LANES - SLOTS,
        pltpu.roll(right, LANES - SLOTS, 1),
        pltpu.roll(own, LANES - SLOTS, 1),
    )
    for dx in range(3):
        place_blocks(near_ref, 2 * dx, before, dx, 0)
        place_blocks(near_ref, 2 * dx + 1, after, dx, 2)
    for c in range(4):
        for bz in range(ZBLOCKS):
            row = (c * ZBLOCKS + bz) * 8 + 1
            own_ref[c, 4 * bz : 4 * bz + 4, :] = own[row : row + 4, :]

    for half in range(2):
        at = slice(8 * half, 8 * half + 8)
        mine = [own_ref[c, at, :] for c in range(3)]
        begun = [begun_ref[k, at, :] for k in range(2 * RADIAL)]
        sums = pair_sums(near_ref, 6, None, mine, half, begun)
        scales = [product_scale(k) / SLOTS for k in range(RADIAL)]
        both = chebyshev_of_products([sums[k] * scales[k] for k in range(RADIAL)])
        ones = chebyshev_of_products([sums[RADIAL + k] * scales[k] for k in range(RADIAL)])
        for k in range(RADIAL):
            feature_ref[k, 8 * half : 8 * half + 8, :] = both[k] - ones[k]
            feature_ref[RADIAL + k, 8 * half : 8 * half + 8, :] = ones[k]

    features = jnp.concatenate(
        [feature_ref[:, bz * 4 + bx, :] for bx in range(4) for bz in range(4)], axis=1
    )
    weight_ref[...] = jnp.zeros(weight_ref.shape, jnp.float32)
    bias_ref[...] = jnp.zeros(bias_ref.shape, jnp.float32)
    for s in range(SPECIES):
        at = s * 16
        weight_ref[0, at : at + NEURONS, : SPECIES * RADIAL] = packed_ref[:15, s, : SPECIES * RADIAL]
        weight_ref[1, at : at + NEURONS, at : at + NEURONS] = packed_ref[15:30, s, :NEURONS]
        weight_ref[2, 2 * s : 2 * s + 2, at : at + NEURONS] = packed_ref[30 + s, :, :NEURONS]
        bias_ref[0:1, at : at + NEURONS] = packed_ref[32, s : s + 1, :NEURONS]
        bias_ref[1:2, at : at + NEURONS] = packed_ref[33, s : s + 1, :NEURONS]
        bias_ref[2:3, 2 * s : 2 * s + 2] = packed_ref[34, s : s + 1, :2]
    diagonal = iota((LANES, LANES), 0) == iota((LANES, LANES), 1)

    def layer(n, x, height):
        bias = jnp.sum(
            jnp.where(diagonal[:height], bias_ref[n : n + 1, :], 0.0), axis=1, keepdims=True
        )
        full = lax.dot_general(
            weight_ref[n, :height, :32], x, TN if n == 1 else NN, precision=lax.Precision.HIGHEST, preferred_element_type=jnp.float32
        )
        return full + bias

    rows = [own_ref[c] for c in range(4)]
    pos_x, pos_y, pos_z, kinds = [row_vector(r) for r in rows]
    answers = layer(2, jnp.tanh(layer(1, jnp.tanh(layer(0, features, 32)), 32)), 8)
    answer = jnp.where(kinds == 0.0, answers[0:2, :], answers[2:4, :])
    charge = answer[1:2, :]
    for bx in range(4):
        for bz in range(4):
            at = (bx * 4 + bz) * LANES
            short_ref[bz, bx : bx + 1, :] = answer[0:1, at : at + LANES]
            charge_ref[bz, bx : bx + 1, :] = charge[:, at : at + LANES]

    along_z = split(spline_weight(z_distance(pos_z)))
    basis = jnp.concatenate([packed_ref[35:, n, :ZPAD] for n in range(2)], axis=0)
    waves = dot3(split(basis), along_z) * charge
    waves_high, waves_low = split(waves)

    per = 4 * LANES
    carry = [None, None]
    for bx in range(4):
        cut = slice(bx * per, (bx + 1) * per)
        ux, uy = 8.0 * pos_x[:, cut], pos_y[:, cut]
        waves_cut = (waves_high[:, cut], waves_low[:, cut])
        weight_y = spline_weight(y_distance(uy, (64, per), iota((64, per), 0)))
        weight_x = spline_weight((iota((16, per), 0) - 1).astype(jnp.float32) - ux)
        for group in range(3):
            product = jnp.concatenate(
                [weight_y * weight_x[4 * group + h : 4 * group + h + 1, :] for h in range(4)], axis=0
            )
            both = dot3(waves_cut, split(product), NT)
            for n in range(2):
                pair = 2 * group + n
                plane = both[:, n * LANES : (n + 1) * LANES]
                if pair < 2 and bx > 0:
                    plane = plane + carry[pair]
                if pair >= 4 and bx < 3:
                    carry[pair - 4] = plane
                else:
                    wire_ref[pl.ds(4 * bx + pair, PLANES, stride=WIRE_ROWS), :] = plane
    tail_x, tail_y = tail_distances(last_blocks(pos_x), last_blocks(pos_y))
    product = spline_weight(tail_x) * spline_weight(tail_y)
    tail = dot3(split(last_blocks(waves)), split(product), NT)
    wire_ref[pl.ds(PATCH_ROWS, PLANES, stride=WIRE_ROWS), :] = tail


def pack_weights(w_first, b_first, w_second, b_second, w_out, b_out):
    parts = [
        w_first.transpose(2, 0, 1),
        w_second.transpose(1, 0, 2),
        w_out.transpose(0, 2, 1),
        b_first[None],
        b_second[None],
        b_out[None],
    ]
    basis = np.zeros((2, PLANES // 2, LANES), np.float32)
    basis[:, :, :ZROWS] = cas(np.arange(PLANES), np.arange(ZROWS), PLANES).reshape(2, PLANES // 2, ZROWS)
    parts.append(basis.transpose(1, 0, 2))
    height = sum(part.shape[0] for part in parts)
    total, first = 0.0, 0
    for part in parts:
        after = height - first - part.shape[0]
        total = total + jnp.pad(part, ((first, after), (0, 0), (0, LANES - part.shape[2])))
        first += part.shape[0]
    return total


def atoms_call(ext, left, right, begun, packed):
    f32 = jnp.float32
    return pl.pallas_call(
        atoms_kernel,
        out_shape=(
            jax.ShapeDtypeStruct((4, 4, LANES), f32),
            jax.ShapeDtypeStruct((4, 4, LANES), f32),
            jax.ShapeDtypeStruct((PLANES * WIRE_ROWS, LANES), f32),
        ),
        scratch_shapes=[
            pltpu.VMEM((6, 4, 24, LANES), f32),
            pltpu.VMEM((4, 16, LANES), f32),
            pltpu.VMEM((SPECIES * RADIAL, 16, LANES), f32),
            pltpu.VMEM((3, 32, LANES), f32),
            pltpu.VMEM((8, LANES), f32),
        ],
        compiler_params=pltpu.CompilerParams(vmem_limit_bytes=VMEM_BYTES),
        name="atoms",
    )(ext, left, right, begun, packed)


def filter_kernel(terms_ref, squares_ref, row_ref, out_ref):
    half = NX // 2
    count = NZ // 4

    def series(square):
        total = None
        for t in range(1, count + 1, 4):
            near = [square + squares_ref[t + n] for n in range(4)]
            parts = [
                (
                    terms_ref[t + n] * near[n + 1] + terms_ref[t + n + 1] * near[n],
                    near[n] * near[n + 1],
                )
                for n in (0, 2)
            ]
            part = (parts[0][0] * parts[1][1] + parts[1][0] * parts[0][1]) / (
                parts[0][1] * parts[1][1]
            )
            total = part if total is None else total + part
        even = square + squares_ref[0]
        extra = terms_ref[0] / jnp.where(even > 0.0, even, 1.0)
        return total + jnp.where(even > 0.0, extra, 0.0)

    square_row, factor_row = row_ref[0:1, :], row_ref[8:9, :]
    middle = row_ref[8:9, half : half + 1]
    edge = series(row_ref[0:8, :] + 0.25) * factor_row * middle
    out_ref[half:, :half] = edge[:, :half]
    first = iota((8, half), 1) == 0
    out_ref[half:, half:] = jnp.where(first, edge[:, half : half + 1], edge[:, :half])
    first_lane = iota((16, half), 1) == 0
    edge = edge[0:1, :half]

    def body(n, _):
        at = pl.multiple_of(n * 16, 16)
        here = at + iota((16, half), 0) == iota((16, half), 1)

        def column(row):
            return jnp.sum(jnp.where(here, row[:, :half], 0.0), axis=1, keepdims=True)

        value = series(square_row[:, :half] + column(square_row)) * factor_row[:, :half] * column(factor_row)
        out_ref[pl.ds(at, 16), :half] = value
        out_ref[pl.ds(at, 16), half:] = jnp.where(first_lane, column(edge), value)
        return 0

    lax.fori_loop(0, half // 16, body, 0)


def filter_tables():
    plane = np.arange(PLANES)[:, None]
    odd = np.arange(1, NZ // 2, 2)
    gaps = np.arange(-(PLANES // 2) + 1, PLANES // 2 + 1)
    window = np.cos(2.0 * np.pi / PLANES * plane * gaps) @ np.cos(
        2.0 * np.pi / NZ * gaps[:, None] * odd
    )
    even = 2 * np.minimum(plane, PLANES - plane)
    wave = np.concatenate([even, np.broadcast_to(odd, (PLANES, odd.size))], axis=1)
    square, factor = axis_factor(wave, NZ)
    count = np.concatenate([np.full((PLANES, 1), float(PLANES)), 2.0 * window], axis=1)
    terms = count * factor / (np.pi * NX * NY * NZ * PLANES)
    return terms.astype(np.float32), square.astype(np.float32)


def filter_call(plane):
    terms, squares = filter_tables()
    square, factor = axis_factor(wave_order(NX), NX)
    row = np.repeat(np.stack([square, factor]), 8, axis=0).astype(np.float32)
    smem = pl.BlockSpec(memory_space=pltpu.SMEM)
    vmem = pl.BlockSpec(memory_space=pltpu.VMEM)
    return pl.pallas_call(
        filter_kernel,
        out_shape=jax.ShapeDtypeStruct((NX // 2 + 8, NY), jnp.float32),
        in_specs=[smem, smem, vmem],
        compiler_params=pltpu.CompilerParams(vmem_limit_bytes=VMEM_BYTES),
        cost_estimate=pl.CostEstimate(flops=20_000_000, bytes_accessed=1 << 20, transcendentals=0),
        name="filter",
    )(
        lax.dynamic_index_in_dim(jnp.asarray(terms), plane, 0, keepdims=False),
        lax.dynamic_index_in_dim(jnp.asarray(squares), plane, 0, keepdims=False),
        row,
    )


def plane_kernel(
    count_x,
    count_y,
    wire_ref,
    filter_ref,
    table_ref,
    out_ref,
    grid_high,
    grid_low,
    result_ref,
    y_high,
    y_low,
    yt_high,
    yt_low,
    x_high,
    x_low,
    xt_high,
    xt_low,
):
    width = x_high.shape[0]

    def fill(high_ref, low_ref, first, value):
        high_ref[first : first + 16, :], low_ref[first : first + 16, :] = split(value)

    def part(name, lanes):
        first, height = TABLE[name]
        return table_ref[first : first + height, :lanes]

    cosine, sine = part("y cos", NY), part("y sin", NY)
    for a in range(32):
        at = slice(a, a + 1)
        fill(y_high, y_low, 16 * a, cosine[at] * part("y cas", NY) + sine[at] * part("y sac", NY))
    cosine, sine = part("x cos", NX), part("x sin", NX)
    plus, minus = part("x cas", NX), part("x sac", NX)
    for x in range(width // 16):
        at = slice(x, x + 1)
        fill(x_high, x_low, 16 * x, cosine * plus[at] + sine * minus[at])
    for name, lanes, high, low in (("yt", NY, yt_high, yt_low), ("xt", width, xt_high, xt_low)):
        cosine, sine = part(name + " cos", lanes), part(name + " sin", lanes)
        plus, minus = part(name + " cas", lanes), part(name + " sac", lanes)
        middle = part(name + " mid", lanes)[0:1]
        for a in range(16):
            at = slice(a, a + 1)
            fill(high, low, 16 * a, cosine[at] * plus + sine[at] * minus)
            value = cosine[at] * minus - sine[at] * plus
            if a == 0:
                value = jnp.where(iota((16, lanes), 0) == 0, middle, value)
            fill(high, low, 256 + 16 * a, value)

    stride = count_y * WIRE_ROWS
    pairs = count_y // 2
    lane = iota((count_x, LANES), 1)
    low_half = lane < 64
    tails = [wire_ref[pl.ds(j * WIRE_ROWS + PATCH_ROWS, count_x, stride=stride), :] for j in range(count_y)]
    own_rows = PATCH_ROWS - 2
    for m in range(pairs):
        before = tails[(2 * m - 1) % count_y]
        between = tails[2 * m]

        def unpacked(x):
            r, h = x // 2, x % 2
            one = wire_ref[pl.ds(2 * m * WIRE_ROWS + r, count_x, stride=stride), :]
            two = wire_ref[pl.ds((2 * m + 1) * WIRE_ROWS + r, count_x, stride=stride), :]
            if h == 0:
                value = jnp.where(low_half, one, pltpu.roll(two, 64, 1))
            else:
                value = jnp.where(low_half, pltpu.roll(one, 64, 1), two)
            first = pltpu.roll(before, (LANES - 3 * x) % LANES, 1) if x else before
            second = pltpu.roll(between, (LANES + 64 - 3 * x) % LANES, 1)
            value = value + jnp.where(lane < 3, first, 0.0)
            return value + jnp.where((lane >= 64) & (lane < 67), second, 0.0)

        for x in range(2 * own_rows):
            value = unpacked(x)
            if x < 3:
                value = value + pltpu.roll(unpacked(x + 2 * own_rows), 1, 0)
            high, low = split(value)
            at = x * count_x
            grid_high[at : at + count_x, m * LANES : (m + 1) * LANES] = high
            grid_low[at : at + count_x, m * LANES : (m + 1) * LANES] = low

    step = split(dot3((grid_high[...], grid_low[...]), (y_high[...], y_low[...])))
    spectrum = dot3((xt_high[...], xt_low[...]), step)
    half = NX // 2
    upper = filter_ref[:half, :]
    lower = jnp.where(iota((half, NY), 0) == 0, filter_ref[half : half + 1, :], upper)
    spectrum = jnp.concatenate([spectrum[:half] * upper, spectrum[half:] * lower], axis=0)
    mean = spectrum[0:1, 0:1]
    first = (iota((8, NX), 0) == 0) & (iota((8, NX), 1) == 0)
    spectrum = jnp.concatenate([jnp.where(first, 0.0, spectrum[:8]), spectrum[8:]], axis=0)
    step = split(dot3((x_high[...], x_low[...]), split(spectrum)))
    result_ref[...] = dot3(step, (yt_high[...], yt_low[...]))

    def result_row(x, m):
        here = x % (2 * own_rows)
        value = result_ref[here * count_x : (here + 1) * count_x, m * LANES : (m + 1) * LANES]
        return pltpu.roll(value, count_x - 1, 0) if x >= 2 * own_rows else value

    for j in range(count_y):
        m = j // 2
        for r in range(PATCH_ROWS):
            even, odd = result_row(2 * r, m), result_row(2 * r + 1, m)
            if j % 2 == 0:
                value = jnp.where(low_half, even, pltpu.roll(odd, 64, 1))
            else:
                value = jnp.where(low_half, pltpu.roll(even, 64, 1), odd)
            out_ref[pl.ds(j * WIRE_ROWS + r, count_x, stride=stride), :] = value
        after = (j + 1) % count_y
        m = after // 2
        tail = jnp.where(lane == LANES - 1, mean, 0.0)
        for x in range(2 * PATCH_ROWS):
            value = result_row(x, m)
            shift = (3 * x - 64 * (after % 2)) % LANES
            if shift:
                value = pltpu.roll(value, shift, 1)
            tail = jnp.where((lane >= 3 * x) & (lane < 3 * x + 3), value, tail)
        out_ref[pl.ds(j * WIRE_ROWS + PATCH_ROWS, count_x, stride=stride), :] = tail


def table_layout():
    heights = {"y cos": 32, "y sin": 32, "y cas": 16, "y sac": 16}
    heights.update({"x cos": 16, "x sin": 16, "x cas": 32, "x sac": 32})
    for name in ("yt", "xt"):
        heights.update({name + " cos": 16, name + " sin": 16, name + " cas": 16, name + " sac": 16, name + " mid": 8})
    layout, first = {}, 0
    for name, height in heights.items():
        layout[name] = (first, height)
        first += height
    return layout, first


TABLE, TABLE_ROWS = table_layout()


def plane_tables(count_x):
    wave, cell = wave_order(NY), np.arange(NY)
    own = np.arange(NX // count_x)
    place = (own[:, None] + (NX // count_x) * np.arange(count_x)).reshape(-1)
    out = np.zeros((TABLE_ROWS, NX), np.float32)

    def put(name, rows, lanes):
        angle = 2.0 * np.pi / NX * (np.outer(rows, lanes) % NX)
        cosine, sine = np.cos(angle), np.sin(angle)
        value = {"cos": cosine, "sin": sine, "cas": cosine + sine, "sac": cosine - sine, "mid": cosine}
        first = TABLE[name][0]
        out[first : first + len(rows), : len(lanes)] = value[name[-3:]]

    sixteen = np.arange(16)
    for kind in ("cos", "sin"):
        put("y " + kind, 16 * np.arange(32), wave)
        put("x " + kind, (NX // count_x) * np.arange(count_x), wave)
        put("yt " + kind, 16 * sixteen, cell)
        put("xt " + kind, 16 * sixteen, place)
    for kind in ("cas", "sac"):
        put("y " + kind, sixteen, wave)
        put("x " + kind, own, wave)
        put("yt " + kind, sixteen, cell)
        put("xt " + kind, sixteen, place)
    put("yt mid", np.array([NY // 2]), cell)
    put("xt mid", np.array([NX // 2]), place)
    return out


def plane_call(wire, table, tables, count_x, count_y):
    return pl.pallas_call(
        functools.partial(plane_kernel, count_x, count_y),
        out_shape=jax.ShapeDtypeStruct((PLANES * WIRE_ROWS, LANES), jnp.float32),
        scratch_shapes=[
            pltpu.VMEM((NX, NY), jnp.bfloat16),
            pltpu.VMEM((NX, NY), jnp.bfloat16),
            pltpu.VMEM((NX, NY), jnp.float32),
            *[pltpu.VMEM((NY, NY), jnp.bfloat16)] * 4,
            *[pltpu.VMEM((NX, NX), jnp.bfloat16)] * 2,
            *[pltpu.VMEM((NX, NX), jnp.bfloat16)] * 2,
        ],
        compiler_params=pltpu.CompilerParams(vmem_limit_bytes=VMEM_BYTES),
        name="plane",
    )(wire, table, tables)


def force_kernel(
    wire_ref, place_ref, short_ref, charge_ref, basis_ref, energy_ref, force_ref, rows_ref
):
    for c in range(3):
        for bz in range(4):
            rows_ref[c, 4 * bz : 4 * bz + 4, :] = place_ref[c, bz, 1:5, :]
    pos_x, pos_y, pos_z = [row_vector(rows_ref[c]) for c in range(3)]
    planes = jnp.concatenate(
        [wire_ref[pl.ds(r, PLANES, stride=WIRE_ROWS), :] for r in range(WIRE_ROWS)], axis=1
    )
    basis = basis_ref[...]
    layers = dot3(split(basis), split(planes))
    mean = lax.dot_general(
        basis,
        planes[:, PATCH_ROWS * LANES :],
        NN,
        precision=lax.Precision.HIGHEST,
        preferred_element_type=jnp.float32,
    )[:, LANES - 1 :]
    high, low = split(layers)
    high, low = high.astype(jnp.float32), low.astype(jnp.float32)
    rest = jnp.zeros((LANES - 3 * ZPAD, layers.shape[1]), jnp.float32)
    columns = jnp.concatenate([high, high, low, rest], axis=0).T.astype(jnp.bfloat16)

    def fold(value):
        out = value[0:8]
        for n in range(1, value.shape[0] // 8):
            out = out + value[8 * n : 8 * n + 8]
        return out

    def z_table(weight, slope):
        high, low = split(jnp.concatenate([weight, slope], axis=1))
        high, low = high.astype(jnp.float32), low.astype(jnp.float32)
        rest = jnp.zeros((LANES - 3 * ZPAD, high.shape[1]), jnp.float32)
        return jnp.concatenate([high, low, high, rest], axis=0).astype(jnp.bfloat16)

    last_x, last_y, last_z = [last_blocks(v) for v in (pos_x, pos_y, pos_z)]
    size = last_x.shape[1]
    layer = (iota((ZPAD, size), 1) // SLOTS) % ZBLOCKS
    last_distance = (iota((ZPAD, size), 0) - 8 * layer - 1).astype(jnp.float32) - 8.0 * last_z
    field = dot(columns[PATCH_ROWS * LANES :, :], z_table(*spline_both(last_distance)))
    here, slope = field[:, :size], field[:, size:]
    tail_x, tail_y = tail_distances(last_x, last_y)
    (tail_x, tail_sx), (tail_y, tail_sy) = spline_both(tail_x), spline_both(tail_y)
    here_y = here * tail_y
    tails = [
        jnp.sum(fold(v), axis=0, keepdims=True)
        for v in (here_y * tail_x, here_y * tail_sx, here * tail_sy * tail_x, slope * tail_y * tail_x)
    ]
    last_lanes = iota((1, LANES), 1) >= LANES - SLOTS

    def tail_of(n, bx, bz):
        at = bx * ZBLOCKS + bz
        half = tails[n][:, (at // 8) * LANES : (at // 8 + 1) * LANES]
        shift = (LANES - SLOTS * (at % 8 + 1)) % LANES
        return jnp.where(last_lanes, pltpu.roll(half, shift, 1) if shift else half, 0.0)

    per = 4 * LANES
    for bx in range(4):
        cut = slice(bx * per, (bx + 1) * per)
        ux, uy = 8.0 * pos_x[:, cut], pos_y[:, cut]
        weight_z, slope_z = spline_both(z_distance(pos_z[:, cut]))
        table = z_table(weight_z, slope_z)
        weight_y, slope_y = spline_both(y_distance(uy, (64, per), iota((64, per), 0)))
        weight_x, slope_x = spline_both((iota((16, per), 0) - 1).astype(jnp.float32) - ux)
        zero = jnp.zeros((8, per), jnp.float32)
        total = [fold(weight_z * mean), zero, zero, fold(slope_z * mean)]
        for pair in range(6):
            r = 4 * bx + pair
            field = dot(columns[r * LANES : (r + 1) * LANES, :], table)
            for h in range(2):
                x = 2 * pair + h
                here = field[64 * h : 64 * h + 64, :per]
                slope = field[64 * h : 64 * h + 64, per:]
                plain = fold(here * weight_y)
                along_y = fold(here * slope_y)
                along_z = fold(slope * weight_y)
                wx, sx = weight_x[x : x + 1, :], slope_x[x : x + 1, :]
                total[0] = total[0] + plain * wx
                total[1] = total[1] + plain * sx
                total[2] = total[2] + along_y * wx
                total[3] = total[3] + along_z * wx
        sums = [jnp.sum(t, axis=0, keepdims=True) for t in total]
        for bz in range(4):
            at = slice(bz * LANES, (bz + 1) * LANES)
            charge = charge_ref[bz, bx : bx + 1, :]
            found = [sums[n][:, at] + tail_of(n, bx, bz) for n in range(4)]
            energy_ref[bz, bx : bx + 1, :] = short_ref[bz, bx : bx + 1, :] + 0.5 * charge * found[0]
            for c in range(3):
                force_ref[c, bz, bx : bx + 1, :] = -charge * found[1 + c]


def force_call(wire, place, short, charge):
    basis = np.zeros((ZPAD, PLANES))
    basis[:ZROWS] = cas(np.arange(ZROWS), np.arange(PLANES), PLANES)
    return pl.pallas_call(
        force_kernel,
        out_shape=(
            jax.ShapeDtypeStruct((4, 4, LANES), jnp.float32),
            jax.ShapeDtypeStruct((3, 4, 4, LANES), jnp.float32),
        ),
        scratch_shapes=[pltpu.VMEM((3, 16, LANES), jnp.float32)],
        compiler_params=pltpu.CompilerParams(vmem_limit_bytes=VMEM_BYTES),
        name="force",
    )(wire, place, short, charge, basis.astype(np.float32))


def ring(size):
    up = [(i, (i + 1) % size) for i in range(size)]
    return up, [(j, i) for i, j in up]


def exchange(wire):
    moved = lax.all_to_all(
        wire.reshape(PLANES, 1, WIRE_ROWS * LANES), ("gx", "gy"), split_axis=0, concat_axis=0, tiled=True
    )
    return moved.reshape(PLANES * WIRE_ROWS, LANES)


def shards(atom_cells, atom_frac, species, *weights):
    count_x, count_y = lax.axis_size("gx"), lax.axis_size("gy")
    assert count_x * count_y == PLANES and atom_cells.shape[1:] == (4, 4, LANES)
    shape = (4,) + species.shape
    is_kind = lax.broadcasted_iota(jnp.int32, shape, 0) == 3
    last = ((0, 1), (0, 0), (0, 0), (0, 0))
    whole = jnp.where(is_kind, jnp.broadcast_to(species, shape), jnp.pad(atom_cells & (BLOCK - 1), last))
    own = (whole.astype(jnp.float32) + jnp.pad(atom_frac, last)) * jnp.where(is_kind, 1.0, 1.0 / BLOCK)
    packed = pack_weights(*weights)
    up, down = ring(count_x)
    before = lax.ppermute(own[:, :, 3:4, :], "gx", up)
    after = lax.ppermute(own[:, :, 0:1, :], "gx", down)
    before, after, packed = lax.optimization_barrier((before, after, packed))
    ext = jnp.concatenate([before, own, after, after, after], axis=2)
    up, down = ring(count_y)
    left = lax.ppermute(ext, "gy", up)
    right = lax.ppermute(ext, "gy", down)
    tables = plane_tables(count_x)
    table = filter_call(lax.axis_index(("gx", "gy")))
    begun = first_pairs_call(ext)
    short, charge, wire = atoms_call(ext, left, right, begun, packed)
    wire = exchange(wire)
    wire = plane_call(wire, table, tables, count_x, count_y)
    wire = exchange(wire)
    energy, force = force_call(wire, ext, short, charge)
    return energy, force, charge


def solution(mesh):
    atoms = P(None, "gx", "gy")
    vectors = P(None, None, "gx", "gy")
    return jax.shard_map(
        shards,
        mesh=mesh,
        in_specs=(vectors, vectors, atoms, P(), P(), P(), P(), P(), P()),
        out_specs=(atoms, vectors, atoms),
        check_vma=False,
    )
```

```python
import functools

import jax
import jax.numpy as jnp
import ml_dtypes
import numpy as np
from jax import lax
from jax.experimental import pallas as pl
from jax.experimental.pallas import tpu as pltpu
from jax.sharding import PartitionSpec as P

NX = 512
NY = 512
NZ = 256
BLOCK = 8
SLOTS = 16
ZBLOCKS = 4
RADIAL = 16
SPECIES = 2
NEURONS = 15
ZROWS = 35
ZPAD = 40
PLANES = 128
EWALD_BETA = 1.0
LANES = 128
PATCH_ROWS = 18
WIRE_ROWS = PATCH_ROWS + 1
NT = (((1,), (1,)), ((), ()))
NN = (((1,), (0,)), ((), ()))
TN = (((0,), (0,)), ((), ()))
VMEM_BYTES = 24 * 1024 * 1024


def high_low(table):
    high = table.astype(ml_dtypes.bfloat16)
    low = (table - high.astype(np.float64)).astype(ml_dtypes.bfloat16)
    return high, low


def split(value):
    high = value.astype(jnp.bfloat16)
    low = (value - high.astype(jnp.float32)).astype(jnp.bfloat16)
    return high, low


def dot(left, right, dims=NN):
    return lax.dot_general(left, right, dims, preferred_element_type=jnp.float32)


def dot3(left, right, dims=NN):
    return (
        dot(left[0], right[0], dims) + dot(left[0], right[1], dims) + dot(left[1], right[0], dims)
    )


def cas(left, right, length):
    angle = 2.0 * np.pi / length * (np.outer(left, right) % length)
    return np.cos(angle) + np.sin(angle)


def wave_order(length):
    half = length // 2
    return np.concatenate([np.arange(half + 1), length - np.arange(1, half)])


def axis_factor(wave, length):
    signed = np.where(wave > length // 2, wave - length, wave) / length
    smooth = 2.0 / 3.0 + np.cos(2.0 * np.pi / length * wave) / 3.0
    return signed**2, np.exp(-((np.pi / EWALD_BETA) ** 2) * signed**2) / smooth**2


def spline_weight(distance):
    away = jnp.abs(distance)
    outer = jnp.maximum(2.0 - away, 0.0)
    inner = jnp.maximum(1.0 - away, 0.0)
    return (outer * outer * outer - 4.0 * (inner * inner * inner)) * (1.0 / 6.0)


def spline_both(distance):
    away = jnp.abs(distance)
    outer = jnp.maximum(2.0 - away, 0.0)
    inner = jnp.maximum(1.0 - away, 0.0)
    outer_sq = outer * outer
    inner_sq = inner * inner
    weight = (outer_sq * outer - 4.0 * (inner_sq * inner)) * (1.0 / 6.0)
    slope = 0.5 * outer_sq - 2.0 * inner_sq
    return weight, jnp.where(distance > 0.0, slope, -slope)


def product_scale(k):
    return float(np.prod([f for n, f in enumerate((-2.0, 8.0, 128.0, 32768.0)) if k >> n & 1]))


def chebyshev_of_products(products):
    out = list(products)
    for top in (2, 4, 8):
        for first in range(0, RADIAL, 2 * top):
            for r in range(1, top):
                out[first + top + r] = 2.0 * out[first + top + r] - out[first + top - r]
    return out


def iota(shape, dim):
    return lax.broadcasted_iota(jnp.int32, shape, dim)


def row_vector(rows):
    return jnp.concatenate(
        [rows[bz * 4 + bx : bz * 4 + bx + 1, :] for bx in range(4) for bz in range(4)], axis=1
    )


def last_blocks(value):
    rows = value.shape[0]
    lane = iota((rows, LANES), 1)
    out = []
    for first in range(0, 16, 8):
        block = jnp.zeros((rows, LANES), value.dtype)
        for n in range(8):
            piece = value[:, (first + n) * LANES : (first + n + 1) * LANES]
            if n < 7:
                piece = pltpu.roll(piece, SLOTS * (n + 1), 1)
            block = jnp.where((lane >= SLOTS * n) & (lane < SLOTS * (n + 1)), piece, block)
        out.append(block)
    return jnp.concatenate(out, axis=1)


def tail_distances(pos_x, pos_y):
    shape = (LANES, pos_x.shape[1])
    place = iota(shape, 0)
    block = iota(shape, 1) // (ZBLOCKS * SLOTS)
    along_x = (place // 3 - 1 - 8 * block).astype(jnp.float32) - 8.0 * pos_x
    along_y = (64 - 1 - 8 * 7 + place % 3).astype(jnp.float32) - 8.0 * pos_y
    return along_x, along_y


def z_distance(pos_z):
    shape = (ZPAD, pos_z.shape[1])
    layer = (iota(shape, 1) // LANES) % ZBLOCKS
    return (iota(shape, 0) - 8 * layer - 1).astype(jnp.float32) - 8.0 * pos_z


def y_distance(pos_y, shape, cell):
    block = (iota(shape, 1) % LANES) // SLOTS
    return (cell - 1 - 8 * block).astype(jnp.float32) - 8.0 * pos_y


def place_rows(near_ref, n, c, bz, value):
    near_ref[n, c, 4 * bz : 4 * bz + 4, :] = value
    if bz == 0:
        near_ref[n, c, 16:20, :] = value
    if bz == ZBLOCKS - 1:
        near_ref[n, c, 20:24, :] = value


def place_blocks(near_ref, n, blocks, dx, dy):
    for c in range(4):
        offset = float((dx - 1, dy - 1, 0, 0)[c])
        for bz in range(ZBLOCKS):
            row = (c * ZBLOCKS + bz) * 8 + dx
            place_rows(near_ref, n, c, bz, blocks[row : row + 4, :] + offset)


def own_rows(own_ref, blocks):
    for c in range(4):
        for bz in range(ZBLOCKS):
            row = (c * ZBLOCKS + bz) * 8 + 1
            own_ref[c, 4 * bz : 4 * bz + 4, :] = blocks[row : row + 4, :]


def pair_sums(near_ref, count, center, own_rows_of, begun_ref, out_ref):
    zero = jnp.zeros((8, LANES), jnp.float32)
    for first, steps in ((0, ((0, 0), (4, 1))), (8, ((8, 0), (4, -1))), (4, ((16, None),))):
        at = slice(first, first + 8)
        mine = [own_rows_of(c, at) for c in range(3)]
        if begun_ref is None or first == 4:
            sums = (zero,) * (2 * RADIAL)
        else:
            sums = tuple(begun_ref[k, at, :] for k in range(2 * RADIAL))
        sums = pair_loop(near_ref, count, center, mine, steps, sums)
        for k in range(2 * RADIAL):
            out_ref[k, at, :] = out_ref[k, at, :] + sums[k] if first == 4 else sums[k]


def pair_loop(near_ref, count, center, mine, steps, sums):
    lane8 = iota((8, LANES), 1)
    mixed = jnp.where(iota((8, LANES), 0) < 4, -1.0, 1.0)

    def body(n, sums):
        sums = list(sums)
        for row, dz in steps:
            near = [near_ref[n, c, row : row + 8, :] for c in range(4)]
            mine_z = mine[2] - (mixed if dz is None else float(dz))
            for turn in range(SLOTS):
                if turn == 0:
                    got = near
                else:
                    index = (lane8 & (LANES - SLOTS)) | ((lane8 + turn) & (SLOTS - 1))
                    got = [jnp.take_along_axis(v, index, axis=1) for v in near]
                gx = got[0] - mine[0]
                gy = got[1] - mine[1]
                gz = got[2] - mine_z
                kind = got[3]
                remain = jnp.maximum(1.0 - (gx * gx + gy * gy + gz * gz), 0.0)
                if turn == 0 and dz == 0 and center is not None:
                    remain = remain * jnp.where(n == center, 0.0, 1.0).astype(jnp.float32)
                half_t = remain - 0.5
                two = half_t * half_t - 1.0 / 8.0
                four = two * two - 1.0 / 128.0
                eight = four * four - 1.0 / 32768.0
                terms = [remain * remain]
                for factor in (half_t, two, four, eight):
                    terms = terms + [term * factor for term in terms]
                for k in range(RADIAL):
                    sums[k] = sums[k] + terms[k]
                    sums[RADIAL + k] = sums[RADIAL + k] + terms[k] * kind
        return tuple(sums)

    return lax.fori_loop(0, count, body, tuple(sums))


def column_pairs_kernel(own_ref, sums_ref, near_ref):
    for c in range(4):
        for bz in range(ZBLOCKS):
            place_rows(near_ref, 0, c, bz, own_ref[c, bz])
    pair_sums(near_ref, 1, 0, lambda c, at: near_ref[0, c, at, :], None, sums_ref)


def column_pairs_call(own):
    return pl.pallas_call(
        column_pairs_kernel,
        out_shape=jax.ShapeDtypeStruct((SPECIES * RADIAL, 16, LANES), jnp.float32),
        scratch_shapes=[pltpu.VMEM((1, 4, 24, LANES), jnp.float32)],
        compiler_params=pltpu.CompilerParams(vmem_limit_bytes=VMEM_BYTES),
        cost_estimate=pl.CostEstimate(flops=8_000_000, bytes_accessed=1 << 18, transcendentals=0),
        name="column_pairs",
    )(own)


def first_pairs_kernel(ext_ref, begun_ref, sums_ref, near_ref, own_ref):
    blocks = ext_ref[...].reshape(LANES, LANES)
    place_blocks(near_ref, 0, blocks, 0, 1)
    place_blocks(near_ref, 1, blocks, 2, 1)
    own_rows(own_ref, blocks)
    pair_sums(near_ref, 2, None, lambda c, at: own_ref[c, at, :], begun_ref, sums_ref)


def first_pairs_call(ext, begun):
    return pl.pallas_call(
        first_pairs_kernel,
        out_shape=jax.ShapeDtypeStruct((SPECIES * RADIAL, 16, LANES), jnp.float32),
        scratch_shapes=[
            pltpu.VMEM((2, 4, 24, LANES), jnp.float32),
            pltpu.VMEM((4, 16, LANES), jnp.float32),
        ],
        compiler_params=pltpu.CompilerParams(vmem_limit_bytes=VMEM_BYTES),
        cost_estimate=pl.CostEstimate(flops=16_000_000, bytes_accessed=1 << 19, transcendentals=0),
        name="first_pairs",
    )(ext, begun)


def atoms_kernel(
    ext_ref,
    left_ref,
    right_ref,
    begun_ref,
    packed_ref,
    short_ref,
    charge_ref,
    wire_ref,
    near_ref,
    own_ref,
    feature_ref,
    weight_ref,
    bias_ref,
):
    lane = iota((LANES, LANES), 1)
    own = ext_ref[...].reshape(LANES, LANES)
    left = left_ref[...].reshape(LANES, LANES)
    right = right_ref[...].reshape(LANES, LANES)
    before = jnp.where(lane < SLOTS, pltpu.roll(left, SLOTS, 1), pltpu.roll(own, SLOTS, 1))
    after = jnp.where(
        lane >= LANES - SLOTS,
        pltpu.roll(right, LANES - SLOTS, 1),
        pltpu.roll(own, LANES - SLOTS, 1),
    )
    for dx in range(3):
        place_blocks(near_ref, 2 * dx, before, dx, 0)
        place_blocks(near_ref, 2 * dx + 1, after, dx, 2)
    own_rows(own_ref, own)

    pair_sums(near_ref, 6, None, lambda c, at: own_ref[c, at, :], begun_ref, feature_ref)
    for half in range(2):
        sums = [feature_ref[k, 8 * half : 8 * half + 8, :] for k in range(2 * RADIAL)]
        scales = [product_scale(k) / SLOTS for k in range(RADIAL)]
        both = chebyshev_of_products([sums[k] * scales[k] for k in range(RADIAL)])
        ones = chebyshev_of_products([sums[RADIAL + k] * scales[k] for k in range(RADIAL)])
        for k in range(RADIAL):
            feature_ref[k, 8 * half : 8 * half + 8, :] = both[k] - ones[k]
            feature_ref[RADIAL + k, 8 * half : 8 * half + 8, :] = ones[k]

    features = jnp.concatenate(
        [feature_ref[:, bz * 4 + bx, :] for bx in range(4) for bz in range(4)], axis=1
    )
    weight_ref[...] = jnp.zeros(weight_ref.shape, jnp.float32)
    bias_ref[...] = jnp.zeros(bias_ref.shape, jnp.float32)
    for s in range(SPECIES):
        at = s * 16
        weight_ref[0, at : at + NEURONS, : SPECIES * RADIAL] = packed_ref[:15, s, : SPECIES * RADIAL]
        weight_ref[1, at : at + NEURONS, at : at + NEURONS] = packed_ref[15:30, s, :NEURONS]
        weight_ref[2, 2 * s : 2 * s + 2, at : at + NEURONS] = packed_ref[30 + s, :, :NEURONS]
        bias_ref[0:1, at : at + NEURONS] = packed_ref[32, s : s + 1, :NEURONS]
        bias_ref[1:2, at : at + NEURONS] = packed_ref[33, s : s + 1, :NEURONS]
        bias_ref[2:3, 2 * s : 2 * s + 2] = packed_ref[34, s : s + 1, :2]
    diagonal = iota((LANES, LANES), 0) == iota((LANES, LANES), 1)

    def layer(n, x, height):
        bias = jnp.sum(
            jnp.where(diagonal[:height], bias_ref[n : n + 1, :], 0.0), axis=1, keepdims=True
        )
        full = lax.dot_general(
            weight_ref[n, :height, :32], x, TN if n == 1 else NN, precision=lax.Precision.HIGHEST, preferred_element_type=jnp.float32
        )
        return full + bias

    rows = [own_ref[c] for c in range(4)]
    pos_x, pos_y, pos_z, kinds = [row_vector(r) for r in rows]
    answers = layer(2, jnp.tanh(layer(1, jnp.tanh(layer(0, features, 32)), 32)), 8)
    answer = jnp.where(kinds == 0.0, answers[0:2, :], answers[2:4, :])
    charge = answer[1:2, :]
    for bx in range(4):
        for bz in range(4):
            at = (bx * 4 + bz) * LANES
            short_ref[bz, bx : bx + 1, :] = answer[0:1, at : at + LANES]
            charge_ref[bz, bx : bx + 1, :] = charge[:, at : at + LANES]

    along_z = split(spline_weight(z_distance(pos_z)))
    basis = jnp.concatenate([packed_ref[35:, n, :ZPAD] for n in range(2)], axis=0)
    waves = dot3(split(basis), along_z) * charge
    waves_high, waves_low = split(waves)

    per = 4 * LANES
    carry = [None, None]
    for bx in range(4):
        cut = slice(bx * per, (bx + 1) * per)
        ux, uy = 8.0 * pos_x[:, cut], pos_y[:, cut]
        waves_cut = (waves_high[:, cut], waves_low[:, cut])
        weight_y = spline_weight(y_distance(uy, (64, per), iota((64, per), 0)))
        weight_x = spline_weight((iota((16, per), 0) - 1).astype(jnp.float32) - ux)
        for group in range(3):
            product = jnp.concatenate(
                [weight_y * weight_x[4 * group + h : 4 * group + h + 1, :] for h in range(4)], axis=0
            )
            both = dot3(waves_cut, split(product), NT)
            for n in range(2):
                pair = 2 * group + n
                plane = both[:, n * LANES : (n + 1) * LANES]
                if pair < 2 and bx > 0:
                    plane = plane + carry[pair]
                if pair >= 4 and bx < 3:
                    carry[pair - 4] = plane
                else:
                    wire_ref[pl.ds(4 * bx + pair, PLANES, stride=WIRE_ROWS), :] = plane
    tail_x, tail_y = tail_distances(last_blocks(pos_x), last_blocks(pos_y))
    product = spline_weight(tail_x) * spline_weight(tail_y)
    tail = dot3(split(last_blocks(waves)), split(product), NT)
    wire_ref[pl.ds(PATCH_ROWS, PLANES, stride=WIRE_ROWS), :] = tail


def pack_weights(w_first, b_first, w_second, b_second, w_out, b_out):
    parts = [
        w_first.transpose(2, 0, 1),
        w_second.transpose(1, 0, 2),
        w_out.transpose(0, 2, 1),
        b_first[None],
        b_second[None],
        b_out[None],
    ]
    basis = np.zeros((2, PLANES // 2, LANES), np.float32)
    basis[:, :, :ZROWS] = cas(np.arange(PLANES), np.arange(ZROWS), PLANES).reshape(2, PLANES // 2, ZROWS)
    parts.append(basis.transpose(1, 0, 2))
    height = sum(part.shape[0] for part in parts)
    total, first = 0.0, 0
    for part in parts:
        after = height - first - part.shape[0]
        total = total + jnp.pad(part, ((first, after), (0, 0), (0, LANES - part.shape[2])))
        first += part.shape[0]
    return total


def atoms_call(ext, left, right, begun, packed):
    f32 = jnp.float32
    return pl.pallas_call(
        atoms_kernel,
        out_shape=(
            jax.ShapeDtypeStruct((4, 4, LANES), f32),
            jax.ShapeDtypeStruct((4, 4, LANES), f32),
            jax.ShapeDtypeStruct((PLANES * WIRE_ROWS, LANES), f32),
        ),
        scratch_shapes=[
            pltpu.VMEM((6, 4, 24, LANES), f32),
            pltpu.VMEM((4, 16, LANES), f32),
            pltpu.VMEM((SPECIES * RADIAL, 16, LANES), f32),
            pltpu.VMEM((3, 32, LANES), f32),
            pltpu.VMEM((8, LANES), f32),
        ],
        compiler_params=pltpu.CompilerParams(vmem_limit_bytes=VMEM_BYTES),
        name="atoms",
    )(ext, left, right, begun, packed)


def filter_kernel(terms_ref, squares_ref, row_ref, out_ref):
    half = NX // 2
    count = NZ // 4

    def series(square):
        total = None
        for t in range(1, count + 1, 4):
            near = [square + squares_ref[t + n] for n in range(4)]
            parts = [
                (
                    terms_ref[t + n] * near[n + 1] + terms_ref[t + n + 1] * near[n],
                    near[n] * near[n + 1],
                )
                for n in (0, 2)
            ]
            part = (parts[0][0] * parts[1][1] + parts[1][0] * parts[0][1]) / (
                parts[0][1] * parts[1][1]
            )
            total = part if total is None else total + part
        even = square + squares_ref[0]
        extra = terms_ref[0] / jnp.where(even > 0.0, even, 1.0)
        return total + jnp.where(even > 0.0, extra, 0.0)

    square_row, factor_row = row_ref[0:1, :], row_ref[8:9, :]
    middle = row_ref[8:9, half : half + 1]
    edge = series(row_ref[0:8, :] + 0.25) * factor_row * middle
    out_ref[half:, :half] = edge[:, :half]
    first = iota((8, half), 1) == 0
    out_ref[half:, half:] = jnp.where(first, edge[:, half : half + 1], edge[:, :half])
    first_lane = iota((16, half), 1) == 0
    edge = edge[0:1, :half]

    def body(n, _):
        at = pl.multiple_of(n * 16, 16)
        here = at + iota((16, half), 0) == iota((16, half), 1)

        def column(row):
            return jnp.sum(jnp.where(here, row[:, :half], 0.0), axis=1, keepdims=True)

        value = series(square_row[:, :half] + column(square_row)) * factor_row[:, :half] * column(factor_row)
        out_ref[pl.ds(at, 16), :half] = value
        out_ref[pl.ds(at, 16), half:] = jnp.where(first_lane, column(edge), value)
        return 0

    lax.fori_loop(0, half // 16, body, 0)


def filter_tables():
    plane = np.arange(PLANES)[:, None]
    odd = np.arange(1, NZ // 2, 2)
    gaps = np.arange(-(PLANES // 2) + 1, PLANES // 2 + 1)
    window = np.cos(2.0 * np.pi / PLANES * plane * gaps) @ np.cos(
        2.0 * np.pi / NZ * gaps[:, None] * odd
    )
    even = 2 * np.minimum(plane, PLANES - plane)
    wave = np.concatenate([even, np.broadcast_to(odd, (PLANES, odd.size))], axis=1)
    square, factor = axis_factor(wave, NZ)
    count = np.concatenate([np.full((PLANES, 1), float(PLANES)), 2.0 * window], axis=1)
    terms = count * factor / (np.pi * NX * NY * NZ * PLANES)
    return terms.astype(np.float32), square.astype(np.float32)


def filter_call(plane):
    terms, squares = filter_tables()
    square, factor = axis_factor(wave_order(NX), NX)
    row = np.repeat(np.stack([square, factor]), 8, axis=0).astype(np.float32)
    smem = pl.BlockSpec(memory_space=pltpu.SMEM)
    vmem = pl.BlockSpec(memory_space=pltpu.VMEM)
    return pl.pallas_call(
        filter_kernel,
        out_shape=jax.ShapeDtypeStruct((NX // 2 + 8, NY), jnp.float32),
        in_specs=[smem, smem, vmem],
        compiler_params=pltpu.CompilerParams(vmem_limit_bytes=VMEM_BYTES),
        cost_estimate=pl.CostEstimate(flops=20_000_000, bytes_accessed=1 << 20, transcendentals=0),
        name="filter",
    )(
        lax.dynamic_index_in_dim(jnp.asarray(terms), plane, 0, keepdims=False),
        lax.dynamic_index_in_dim(jnp.asarray(squares), plane, 0, keepdims=False),
        row,
    )


def plane_kernel(
    count_x,
    count_y,
    wire_ref,
    filter_ref,
    table_ref,
    out_ref,
    grid_high,
    grid_low,
    result_ref,
    y_high,
    y_low,
    yt_high,
    yt_low,
    x_high,
    x_low,
    xt_high,
    xt_low,
):
    width = x_high.shape[0]

    def fill(high_ref, low_ref, first, value):
        high_ref[first : first + 16, :], low_ref[first : first + 16, :] = split(value)

    def part(name, lanes):
        first, height = TABLE[name]
        return table_ref[first : first + height, :lanes]

    cosine, sine = part("y cos", NY), part("y sin", NY)
    for a in range(32):
        at = slice(a, a + 1)
        fill(y_high, y_low, 16 * a, cosine[at] * part("y cas", NY) + sine[at] * part("y sac", NY))
    cosine, sine = part("x cos", NX), part("x sin", NX)
    plus, minus = part("x cas", NX), part("x sac", NX)
    for x in range(width // 16):
        at = slice(x, x + 1)
        fill(x_high, x_low, 16 * x, cosine * plus[at] + sine * minus[at])
    for name, lanes, high, low in (("yt", NY, yt_high, yt_low), ("xt", width, xt_high, xt_low)):
        cosine, sine = part(name + " cos", lanes), part(name + " sin", lanes)
        plus, minus = part(name + " cas", lanes), part(name + " sac", lanes)
        middle = part(name + " mid", lanes)[0:1]
        for a in range(16):
            at = slice(a, a + 1)
            fill(high, low, 16 * a, cosine[at] * plus + sine[at] * minus)
            value = cosine[at] * minus - sine[at] * plus
            if a == 0:
                value = jnp.where(iota((16, lanes), 0) == 0, middle, value)
            fill(high, low, 256 + 16 * a, value)

    stride = count_y * WIRE_ROWS
    pairs = count_y // 2
    lane = iota((count_x, LANES), 1)
    low_half = lane < 64
    tails = [wire_ref[pl.ds(j * WIRE_ROWS + PATCH_ROWS, count_x, stride=stride), :] for j in range(count_y)]
    own_rows = PATCH_ROWS - 2
    for m in range(pairs):
        before = tails[(2 * m - 1) % count_y]
        between = tails[2 * m]

        def unpacked(x):
            r, h = x // 2, x % 2
            one = wire_ref[pl.ds(2 * m * WIRE_ROWS + r, count_x, stride=stride), :]
            two = wire_ref[pl.ds((2 * m + 1) * WIRE_ROWS + r, count_x, stride=stride), :]
            if h == 0:
                value = jnp.where(low_half, one, pltpu.roll(two, 64, 1))
            else:
                value = jnp.where(low_half, pltpu.roll(one, 64, 1), two)
            first = pltpu.roll(before, (LANES - 3 * x) % LANES, 1) if x else before
            second = pltpu.roll(between, (LANES + 64 - 3 * x) % LANES, 1)
            value = value + jnp.where(lane < 3, first, 0.0)
            return value + jnp.where((lane >= 64) & (lane < 67), second, 0.0)

        for x in range(2 * own_rows):
            value = unpacked(x)
            if x < 3:
                value = value + pltpu.roll(unpacked(x + 2 * own_rows), 1, 0)
            high, low = split(value)
            at = x * count_x
            grid_high[at : at + count_x, m * LANES : (m + 1) * LANES] = high
            grid_low[at : at + count_x, m * LANES : (m + 1) * LANES] = low

    step = split(dot3((grid_high[...], grid_low[...]), (y_high[...], y_low[...])))
    spectrum = dot3((xt_high[...], xt_low[...]), step)
    half = NX // 2
    upper = filter_ref[:half, :]
    lower = jnp.where(iota((half, NY), 0) == 0, filter_ref[half : half + 1, :], upper)
    spectrum = jnp.concatenate([spectrum[:half] * upper, spectrum[half:] * lower], axis=0)
    mean = spectrum[0:1, 0:1]
    first = (iota((8, NX), 0) == 0) & (iota((8, NX), 1) == 0)
    spectrum = jnp.concatenate([jnp.where(first, 0.0, spectrum[:8]), spectrum[8:]], axis=0)
    step = split(dot3((x_high[...], x_low[...]), split(spectrum)))
    result_ref[...] = dot3(step, (yt_high[...], yt_low[...]))

    def result_row(x, m):
        here = x % (2 * own_rows)
        value = result_ref[here * count_x : (here + 1) * count_x, m * LANES : (m + 1) * LANES]
        return pltpu.roll(value, count_x - 1, 0) if x >= 2 * own_rows else value

    for j in range(count_y):
        m = j // 2
        for r in range(PATCH_ROWS):
            even, odd = result_row(2 * r, m), result_row(2 * r + 1, m)
            if j % 2 == 0:
                value = jnp.where(low_half, even, pltpu.roll(odd, 64, 1))
            else:
                value = jnp.where(low_half, pltpu.roll(even, 64, 1), odd)
            out_ref[pl.ds(j * WIRE_ROWS + r, count_x, stride=stride), :] = value
        after = (j + 1) % count_y
        m = after // 2
        tail = jnp.where(lane == LANES - 1, mean, 0.0)
        for x in range(2 * PATCH_ROWS):
            value = result_row(x, m)
            shift = (3 * x - 64 * (after % 2)) % LANES
            if shift:
                value = pltpu.roll(value, shift, 1)
            tail = jnp.where((lane >= 3 * x) & (lane < 3 * x + 3), value, tail)
        out_ref[pl.ds(j * WIRE_ROWS + PATCH_ROWS, count_x, stride=stride), :] = tail


def table_layout():
    heights = {"y cos": 32, "y sin": 32, "y cas": 16, "y sac": 16}
    heights.update({"x cos": 16, "x sin": 16, "x cas": 32, "x sac": 32})
    for name in ("yt", "xt"):
        heights.update({name + " cos": 16, name + " sin": 16, name + " cas": 16, name + " sac": 16, name + " mid": 8})
    layout, first = {}, 0
    for name, height in heights.items():
        layout[name] = (first, height)
        first += height
    return layout, first


TABLE, TABLE_ROWS = table_layout()


def plane_tables(count_x):
    wave, cell = wave_order(NY), np.arange(NY)
    own = np.arange(NX // count_x)
    place = (own[:, None] + (NX // count_x) * np.arange(count_x)).reshape(-1)
    out = np.zeros((TABLE_ROWS, NX), np.float32)

    def put(name, rows, lanes):
        angle = 2.0 * np.pi / NX * (np.outer(rows, lanes) % NX)
        cosine, sine = np.cos(angle), np.sin(angle)
        value = {"cos": cosine, "sin": sine, "cas": cosine + sine, "sac": cosine - sine, "mid": cosine}
        first = TABLE[name][0]
        out[first : first + len(rows), : len(lanes)] = value[name[-3:]]

    sixteen = np.arange(16)
    for kind in ("cos", "sin"):
        put("y " + kind, 16 * np.arange(32), wave)
        put("x " + kind, (NX // count_x) * np.arange(count_x), wave)
        put("yt " + kind, 16 * sixteen, cell)
        put("xt " + kind, 16 * sixteen, place)
    for kind in ("cas", "sac"):
        put("y " + kind, sixteen, wave)
        put("x " + kind, own, wave)
        put("yt " + kind, sixteen, cell)
        put("xt " + kind, sixteen, place)
    put("yt mid", np.array([NY // 2]), cell)
    put("xt mid", np.array([NX // 2]), place)
    return out


def plane_call(wire, table, tables, count_x, count_y):
    return pl.pallas_call(
        functools.partial(plane_kernel, count_x, count_y),
        out_shape=jax.ShapeDtypeStruct((PLANES * WIRE_ROWS, LANES), jnp.float32),
        scratch_shapes=[
            pltpu.VMEM((NX, NY), jnp.bfloat16),
            pltpu.VMEM((NX, NY), jnp.bfloat16),
            pltpu.VMEM((NX, NY), jnp.float32),
            *[pltpu.VMEM((NY, NY), jnp.bfloat16)] * 4,
            *[pltpu.VMEM((NX, NX), jnp.bfloat16)] * 2,
            *[pltpu.VMEM((NX, NX), jnp.bfloat16)] * 2,
        ],
        compiler_params=pltpu.CompilerParams(vmem_limit_bytes=VMEM_BYTES),
        name="plane",
    )(wire, table, tables)


def force_kernel(
    wire_ref, place_ref, short_ref, charge_ref, basis_ref, energy_ref, force_ref, rows_ref
):
    for c in range(3):
        for bz in range(4):
            rows_ref[c, 4 * bz : 4 * bz + 4, :] = place_ref[c, bz, 1:5, :]
    pos_x, pos_y, pos_z = [row_vector(rows_ref[c]) for c in range(3)]
    planes = jnp.concatenate(
        [wire_ref[pl.ds(r, PLANES, stride=WIRE_ROWS), :] for r in range(WIRE_ROWS)], axis=1
    )
    basis = basis_ref[...]
    layers = dot3(split(basis), split(planes))
    mean = lax.dot_general(
        basis,
        planes[:, PATCH_ROWS * LANES :],
        NN,
        precision=lax.Precision.HIGHEST,
        preferred_element_type=jnp.float32,
    )[:, LANES - 1 :]
    high, low = split(layers)
    high, low = high.astype(jnp.float32), low.astype(jnp.float32)
    rest = jnp.zeros((LANES - 3 * ZPAD, layers.shape[1]), jnp.float32)
    columns = jnp.concatenate([high, high, low, rest], axis=0).T.astype(jnp.bfloat16)

    def fold(value):
        out = value[0:8]
        for n in range(1, value.shape[0] // 8):
            out = out + value[8 * n : 8 * n + 8]
        return out

    def z_table(weight, slope):
        high, low = split(jnp.concatenate([weight, slope], axis=1))
        high, low = high.astype(jnp.float32), low.astype(jnp.float32)
        rest = jnp.zeros((LANES - 3 * ZPAD, high.shape[1]), jnp.float32)
        return jnp.concatenate([high, low, high, rest], axis=0).astype(jnp.bfloat16)

    last_x, last_y, last_z = [last_blocks(v) for v in (pos_x, pos_y, pos_z)]
    size = last_x.shape[1]
    layer = (iota((ZPAD, size), 1) // SLOTS) % ZBLOCKS
    last_distance = (iota((ZPAD, size), 0) - 8 * layer - 1).astype(jnp.float32) - 8.0 * last_z
    field = dot(columns[PATCH_ROWS * LANES :, :], z_table(*spline_both(last_distance)))
    here, slope = field[:, :size], field[:, size:]
    tail_x, tail_y = tail_distances(last_x, last_y)
    (tail_x, tail_sx), (tail_y, tail_sy) = spline_both(tail_x), spline_both(tail_y)
    here_y = here * tail_y
    tails = [
        jnp.sum(fold(v), axis=0, keepdims=True)
        for v in (here_y * tail_x, here_y * tail_sx, here * tail_sy * tail_x, slope * tail_y * tail_x)
    ]
    last_lanes = iota((1, LANES), 1) >= LANES - SLOTS

    def tail_of(n, bx, bz):
        at = bx * ZBLOCKS + bz
        half = tails[n][:, (at // 8) * LANES : (at // 8 + 1) * LANES]
        shift = (LANES - SLOTS * (at % 8 + 1)) % LANES
        return jnp.where(last_lanes, pltpu.roll(half, shift, 1) if shift else half, 0.0)

    per = 4 * LANES
    for bx in range(4):
        cut = slice(bx * per, (bx + 1) * per)
        ux, uy = 8.0 * pos_x[:, cut], pos_y[:, cut]
        weight_z, slope_z = spline_both(z_distance(pos_z[:, cut]))
        table = z_table(weight_z, slope_z)
        weight_y, slope_y = spline_both(y_distance(uy, (64, per), iota((64, per), 0)))
        weight_x, slope_x = spline_both((iota((16, per), 0) - 1).astype(jnp.float32) - ux)
        zero = jnp.zeros((8, per), jnp.float32)
        total = [fold(weight_z * mean), zero, zero, fold(slope_z * mean)]
        for pair in range(6):
            r = 4 * bx + pair
            field = dot(columns[r * LANES : (r + 1) * LANES, :], table)
            for h in range(2):
                x = 2 * pair + h
                here = field[64 * h : 64 * h + 64, :per]
                slope = field[64 * h : 64 * h + 64, per:]
                plain = fold(here * weight_y)
                along_y = fold(here * slope_y)
                along_z = fold(slope * weight_y)
                wx, sx = weight_x[x : x + 1, :], slope_x[x : x + 1, :]
                total[0] = total[0] + plain * wx
                total[1] = total[1] + plain * sx
                total[2] = total[2] + along_y * wx
                total[3] = total[3] + along_z * wx
        sums = [jnp.sum(t, axis=0, keepdims=True) for t in total]
        for bz in range(4):
            at = slice(bz * LANES, (bz + 1) * LANES)
            charge = charge_ref[bz, bx : bx + 1, :]
            found = [sums[n][:, at] + tail_of(n, bx, bz) for n in range(4)]
            energy_ref[bz, bx : bx + 1, :] = short_ref[bz, bx : bx + 1, :] + 0.5 * charge * found[0]
            for c in range(3):
                force_ref[c, bz, bx : bx + 1, :] = -charge * found[1 + c]


def force_call(wire, place, short, charge):
    basis = np.zeros((ZPAD, PLANES))
    basis[:ZROWS] = cas(np.arange(ZROWS), np.arange(PLANES), PLANES)
    return pl.pallas_call(
        force_kernel,
        out_shape=(
            jax.ShapeDtypeStruct((4, 4, LANES), jnp.float32),
            jax.ShapeDtypeStruct((3, 4, 4, LANES), jnp.float32),
        ),
        scratch_shapes=[pltpu.VMEM((3, 16, LANES), jnp.float32)],
        compiler_params=pltpu.CompilerParams(vmem_limit_bytes=VMEM_BYTES),
        name="force",
    )(wire, place, short, charge, basis.astype(np.float32))


def ring(size):
    up = [(i, (i + 1) % size) for i in range(size)]
    return up, [(j, i) for i, j in up]


def exchange(wire):
    moved = lax.all_to_all(
        wire.reshape(PLANES, 1, WIRE_ROWS * LANES), ("gx", "gy"), split_axis=0, concat_axis=0, tiled=True
    )
    return moved.reshape(PLANES * WIRE_ROWS, LANES)


def shards(atom_cells, atom_frac, species, *weights):
    count_x, count_y = lax.axis_size("gx"), lax.axis_size("gy")
    assert count_x * count_y == PLANES and atom_cells.shape[1:] == (4, 4, LANES)
    shape = (4,) + species.shape
    is_kind = lax.broadcasted_iota(jnp.int32, shape, 0) == 3
    last = ((0, 1), (0, 0), (0, 0), (0, 0))
    whole = jnp.where(is_kind, jnp.broadcast_to(species, shape), jnp.pad(atom_cells & (BLOCK - 1), last))
    own = (whole.astype(jnp.float32) + jnp.pad(atom_frac, last)) * jnp.where(is_kind, 1.0, 1.0 / BLOCK)
    packed = pack_weights(*weights)
    up, down = ring(count_x)
    before = lax.ppermute(own[:, :, 3:4, :], "gx", up)
    after = lax.ppermute(own[:, :, 0:1, :], "gx", down)
    begun = column_pairs_call(own)
    before, after, packed, begun = lax.optimization_barrier((before, after, packed, begun))
    ext = jnp.concatenate([before, own, after, after, after], axis=2)
    up, down = ring(count_y)
    left = lax.ppermute(ext, "gy", up)
    right = lax.ppermute(ext, "gy", down)
    tables = plane_tables(count_x)
    table = filter_call(lax.axis_index(("gx", "gy")))
    begun = first_pairs_call(ext, begun)
    short, charge, wire = atoms_call(ext, left, right, begun, packed)
    wire = exchange(wire)
    wire = plane_call(wire, table, tables, count_x, count_y)
    wire = exchange(wire)
    energy, force = force_call(wire, ext, short, charge)
    return energy, force, charge


def solution(mesh):
    atoms = P(None, "gx", "gy")
    vectors = P(None, None, "gx", "gy")
    return jax.shard_map(
        shards,
        mesh=mesh,
        in_specs=(vectors, vectors, atoms, P(), P(), P(), P(), P(), P()),
        out_specs=(atoms, vectors, atoms),
        check_vma=False,
    )
```

```python
import functools

import jax
import jax.numpy as jnp
import ml_dtypes
import numpy as np
from jax import lax
from jax.experimental import pallas as pl
from jax.experimental.pallas import tpu as pltpu
from jax.sharding import PartitionSpec as P

NX = 512
NY = 512
NZ = 256
BLOCK = 8
SLOTS = 16
ZBLOCKS = 4
RADIAL = 16
SPECIES = 2
NEURONS = 15
ZROWS = 35
ZPAD = 40
PLANES = 128
EWALD_BETA = 1.0
LANES = 128
PATCH_ROWS = 18
WIRE_ROWS = PATCH_ROWS + 1
NT = (((1,), (1,)), ((), ()))
NN = (((1,), (0,)), ((), ()))
TN = (((0,), (0,)), ((), ()))
VMEM_BYTES = 24 * 1024 * 1024


def high_low(table):
    high = table.astype(ml_dtypes.bfloat16)
    low = (table - high.astype(np.float64)).astype(ml_dtypes.bfloat16)
    return high, low


def split(value):
    high = value.astype(jnp.bfloat16)
    low = (value - high.astype(jnp.float32)).astype(jnp.bfloat16)
    return high, low


def dot(left, right, dims=NN):
    return lax.dot_general(left, right, dims, preferred_element_type=jnp.float32)


def dot3(left, right, dims=NN):
    return (
        dot(left[0], right[0], dims) + dot(left[0], right[1], dims) + dot(left[1], right[0], dims)
    )


def cas(left, right, length):
    angle = 2.0 * np.pi / length * (np.outer(left, right) % length)
    return np.cos(angle) + np.sin(angle)


def wave_order(length):
    half = length // 2
    return np.concatenate([np.arange(half + 1), length - np.arange(1, half)])


def axis_factor(wave, length):
    signed = np.where(wave > length // 2, wave - length, wave) / length
    smooth = 2.0 / 3.0 + np.cos(2.0 * np.pi / length * wave) / 3.0
    return signed**2, np.exp(-((np.pi / EWALD_BETA) ** 2) * signed**2) / smooth**2


def spline_weight(distance):
    away = jnp.abs(distance)
    outer = jnp.maximum(2.0 - away, 0.0)
    inner = jnp.maximum(1.0 - away, 0.0)
    return (outer * outer * outer - 4.0 * (inner * inner * inner)) * (1.0 / 6.0)


def spline_both(distance):
    away = jnp.abs(distance)
    outer = jnp.maximum(2.0 - away, 0.0)
    inner = jnp.maximum(1.0 - away, 0.0)
    outer_sq = outer * outer
    inner_sq = inner * inner
    weight = (outer_sq * outer - 4.0 * (inner_sq * inner)) * (1.0 / 6.0)
    slope = 0.5 * outer_sq - 2.0 * inner_sq
    return weight, jnp.where(distance > 0.0, slope, -slope)


def product_scale(k):
    return float(np.prod([f for n, f in enumerate((-2.0, 8.0, 128.0, 32768.0)) if k >> n & 1]))


def chebyshev_of_products(products):
    out = list(products)
    for top in (2, 4, 8):
        for first in range(0, RADIAL, 2 * top):
            for r in range(1, top):
                out[first + top + r] = 2.0 * out[first + top + r] - out[first + top - r]
    return out


def iota(shape, dim):
    return lax.broadcasted_iota(jnp.int32, shape, dim)


def row_vector(rows):
    return jnp.concatenate(
        [rows[bz * 4 + bx : bz * 4 + bx + 1, :] for bx in range(4) for bz in range(4)], axis=1
    )


def last_blocks(value):
    rows = value.shape[0]
    lane = iota((rows, LANES), 1)
    out = []
    for first in range(0, 16, 8):
        block = jnp.zeros((rows, LANES), value.dtype)
        for n in range(8):
            piece = value[:, (first + n) * LANES : (first + n + 1) * LANES]
            if n < 7:
                piece = pltpu.roll(piece, SLOTS * (n + 1), 1)
            block = jnp.where((lane >= SLOTS * n) & (lane < SLOTS * (n + 1)), piece, block)
        out.append(block)
    return jnp.concatenate(out, axis=1)


def tail_distances(pos_x, pos_y):
    shape = (LANES, pos_x.shape[1])
    place = iota(shape, 0)
    block = iota(shape, 1) // (ZBLOCKS * SLOTS)
    along_x = (place // 3 - 1 - 8 * block).astype(jnp.float32) - 8.0 * pos_x
    along_y = (64 - 1 - 8 * 7 + place % 3).astype(jnp.float32) - 8.0 * pos_y
    return along_x, along_y


def z_distance(pos_z):
    shape = (ZPAD, pos_z.shape[1])
    layer = (iota(shape, 1) // LANES) % ZBLOCKS
    return (iota(shape, 0) - 8 * layer - 1).astype(jnp.float32) - 8.0 * pos_z


def y_distance(pos_y, shape, cell):
    block = (iota(shape, 1) % LANES) // SLOTS
    return (cell - 1 - 8 * block).astype(jnp.float32) - 8.0 * pos_y


def place_rows(near_ref, n, c, bz, value):
    near_ref[n, c, 4 * bz : 4 * bz + 4, :] = value
    if bz == 0:
        near_ref[n, c, 16:20, :] = value
    if bz == ZBLOCKS - 1:
        near_ref[n, c, 20:24, :] = value


def place_blocks(near_ref, n, blocks, dx, dy):
    for c in range(4):
        offset = float((dx - 1, dy - 1, 0, 0)[c])
        for bz in range(ZBLOCKS):
            row = (c * ZBLOCKS + bz) * 8 + dx
            place_rows(near_ref, n, c, bz, blocks[row : row + 4, :] + offset)


def own_rows(own_ref, blocks):
    for c in range(4):
        for bz in range(ZBLOCKS):
            row = (c * ZBLOCKS + bz) * 8 + 1
            own_ref[c, 4 * bz : 4 * bz + 4, :] = blocks[row : row + 4, :]


def pair_sums(near_ref, count, center, own_rows_of, begun_ref, out_ref):
    zero = jnp.zeros((8, LANES), jnp.float32)
    for first, steps in ((0, ((0, 0), (4, 1))), (8, ((8, 0), (4, -1))), (4, ((16, None),))):
        at = slice(first, first + 8)
        mine = [own_rows_of(c, at) for c in range(3)]
        if begun_ref is None or first == 4:
            sums = (zero,) * (2 * RADIAL)
        else:
            sums = tuple(begun_ref[k, at, :] for k in range(2 * RADIAL))
        sums = pair_loop(near_ref, count, center, mine, steps, sums)
        for k in range(2 * RADIAL):
            out_ref[k, at, :] = out_ref[k, at, :] + sums[k] if first == 4 else sums[k]


def pair_loop(near_ref, count, center, mine, steps, sums):
    lane8 = iota((8, LANES), 1)
    mixed = jnp.where(iota((8, LANES), 0) < 4, -1.0, 1.0)

    def body(n, sums):
        sums = list(sums)
        for row, dz in steps:
            near = [near_ref[n, c, row : row + 8, :] for c in range(4)]
            mine_z = mine[2] - (mixed if dz is None else float(dz))
            for turn in range(SLOTS):
                if turn == 0:
                    got = near
                else:
                    index = (lane8 & (LANES - SLOTS)) | ((lane8 + turn) & (SLOTS - 1))
                    got = [jnp.take_along_axis(v, index, axis=1) for v in near]
                gx = got[0] - mine[0]
                gy = got[1] - mine[1]
                gz = got[2] - mine_z
                kind = got[3]
                remain = jnp.maximum(1.0 - (gx * gx + gy * gy + gz * gz), 0.0)
                if turn == 0 and dz == 0 and center is not None:
                    remain = remain * jnp.where(n == center, 0.0, 1.0).astype(jnp.float32)
                half_t = remain - 0.5
                two = half_t * half_t - 1.0 / 8.0
                four = two * two - 1.0 / 128.0
                eight = four * four - 1.0 / 32768.0
                terms = [remain * remain]
                for factor in (half_t, two, four, eight):
                    terms = terms + [term * factor for term in terms]
                for k in range(RADIAL):
                    sums[k] = sums[k] + terms[k]
                    sums[RADIAL + k] = sums[RADIAL + k] + terms[k] * kind
        return tuple(sums)

    unroll = 2 if len(steps) == 1 and count % 2 == 0 else 1
    return lax.fori_loop(0, count, body, tuple(sums), unroll=unroll)


def column_pairs_kernel(own_ref, sums_ref, near_ref):
    for c in range(4):
        for bz in range(ZBLOCKS):
            place_rows(near_ref, 0, c, bz, own_ref[c, bz])
    pair_sums(near_ref, 1, 0, lambda c, at: near_ref[0, c, at, :], None, sums_ref)


def column_pairs_call(own):
    return pl.pallas_call(
        column_pairs_kernel,
        out_shape=jax.ShapeDtypeStruct((SPECIES * RADIAL, 16, LANES), jnp.float32),
        scratch_shapes=[pltpu.VMEM((1, 4, 24, LANES), jnp.float32)],
        compiler_params=pltpu.CompilerParams(vmem_limit_bytes=VMEM_BYTES),
        cost_estimate=pl.CostEstimate(flops=8_000_000, bytes_accessed=1 << 18, transcendentals=0),
        name="column_pairs",
    )(own)


def first_pairs_kernel(ext_ref, begun_ref, sums_ref, near_ref, own_ref):
    blocks = ext_ref[...].reshape(LANES, LANES)
    place_blocks(near_ref, 0, blocks, 0, 1)
    place_blocks(near_ref, 1, blocks, 2, 1)
    own_rows(own_ref, blocks)
    pair_sums(near_ref, 2, None, lambda c, at: own_ref[c, at, :], begun_ref, sums_ref)


def first_pairs_call(ext, begun):
    return pl.pallas_call(
        first_pairs_kernel,
        out_shape=jax.ShapeDtypeStruct((SPECIES * RADIAL, 16, LANES), jnp.float32),
        scratch_shapes=[
            pltpu.VMEM((2, 4, 24, LANES), jnp.float32),
            pltpu.VMEM((4, 16, LANES), jnp.float32),
        ],
        compiler_params=pltpu.CompilerParams(vmem_limit_bytes=VMEM_BYTES),
        cost_estimate=pl.CostEstimate(flops=16_000_000, bytes_accessed=1 << 19, transcendentals=0),
        name="first_pairs",
    )(ext, begun)


def atoms_kernel(
    ext_ref,
    left_ref,
    right_ref,
    begun_ref,
    packed_ref,
    short_ref,
    charge_ref,
    wire_ref,
    near_ref,
    own_ref,
    feature_ref,
    weight_ref,
    bias_ref,
):
    lane = iota((LANES, LANES), 1)
    own = ext_ref[...].reshape(LANES, LANES)
    left = left_ref[...].reshape(LANES, LANES)
    right = right_ref[...].reshape(LANES, LANES)
    before = jnp.where(lane < SLOTS, pltpu.roll(left, SLOTS, 1), pltpu.roll(own, SLOTS, 1))
    after = jnp.where(
        lane >= LANES - SLOTS,
        pltpu.roll(right, LANES - SLOTS, 1),
        pltpu.roll(own, LANES - SLOTS, 1),
    )
    for dx in range(3):
        place_blocks(near_ref, 2 * dx, before, dx, 0)
        place_blocks(near_ref, 2 * dx + 1, after, dx, 2)
    own_rows(own_ref, own)

    pair_sums(near_ref, 6, None, lambda c, at: own_ref[c, at, :], begun_ref, feature_ref)
    for half in range(2):
        sums = [feature_ref[k, 8 * half : 8 * half + 8, :] for k in range(2 * RADIAL)]
        scales = [product_scale(k) / SLOTS for k in range(RADIAL)]
        both = chebyshev_of_products([sums[k] * scales[k] for k in range(RADIAL)])
        ones = chebyshev_of_products([sums[RADIAL + k] * scales[k] for k in range(RADIAL)])
        for k in range(RADIAL):
            feature_ref[k, 8 * half : 8 * half + 8, :] = both[k] - ones[k]
            feature_ref[RADIAL + k, 8 * half : 8 * half + 8, :] = ones[k]

    features = jnp.concatenate(
        [feature_ref[:, bz * 4 + bx, :] for bx in range(4) for bz in range(4)], axis=1
    )
    weight_ref[...] = jnp.zeros(weight_ref.shape, jnp.float32)
    bias_ref[...] = jnp.zeros(bias_ref.shape, jnp.float32)
    for s in range(SPECIES):
        at = s * 16
        weight_ref[0, at : at + NEURONS, : SPECIES * RADIAL] = packed_ref[:15, s, : SPECIES * RADIAL]
        weight_ref[1, at : at + NEURONS, at : at + NEURONS] = packed_ref[15:30, s, :NEURONS]
        weight_ref[2, 2 * s : 2 * s + 2, at : at + NEURONS] = packed_ref[30 + s, :, :NEURONS]
        bias_ref[0:1, at : at + NEURONS] = packed_ref[32, s : s + 1, :NEURONS]
        bias_ref[1:2, at : at + NEURONS] = packed_ref[33, s : s + 1, :NEURONS]
        bias_ref[2:3, 2 * s : 2 * s + 2] = packed_ref[34, s : s + 1, :2]
    diagonal = iota((LANES, LANES), 0) == iota((LANES, LANES), 1)

    def layer(n, x, height):
        bias = jnp.sum(
            jnp.where(diagonal[:height], bias_ref[n : n + 1, :], 0.0), axis=1, keepdims=True
        )
        full = lax.dot_general(
            weight_ref[n, :height, :32], x, TN if n == 1 else NN, precision=lax.Precision.HIGHEST, preferred_element_type=jnp.float32
        )
        return full + bias

    rows = [own_ref[c] for c in range(4)]
    pos_x, pos_y, pos_z, kinds = [row_vector(r) for r in rows]
    answers = layer(2, jnp.tanh(layer(1, jnp.tanh(layer(0, features, 32)), 32)), 8)
    answer = jnp.where(kinds == 0.0, answers[0:2, :], answers[2:4, :])
    charge = answer[1:2, :]
    for bx in range(4):
        for bz in range(4):
            at = (bx * 4 + bz) * LANES
            short_ref[bz, bx : bx + 1, :] = answer[0:1, at : at + LANES]
            charge_ref[bz, bx : bx + 1, :] = charge[:, at : at + LANES]

    along_z = split(spline_weight(z_distance(pos_z)))
    basis = jnp.concatenate([packed_ref[35:, n, :ZPAD] for n in range(2)], axis=0)
    waves = dot3(split(basis), along_z) * charge
    waves_high, waves_low = split(waves)

    per = 4 * LANES
    carry = [None, None]
    for bx in range(4):
        cut = slice(bx * per, (bx + 1) * per)
        ux, uy = 8.0 * pos_x[:, cut], pos_y[:, cut]
        waves_cut = (waves_high[:, cut], waves_low[:, cut])
        weight_y = spline_weight(y_distance(uy, (64, per), iota((64, per), 0)))
        weight_x = spline_weight((iota((16, per), 0) - 1).astype(jnp.float32) - ux)
        for group in range(3):
            product = jnp.concatenate(
                [weight_y * weight_x[4 * group + h : 4 * group + h + 1, :] for h in range(4)], axis=0
            )
            both = dot3(waves_cut, split(product), NT)
            for n in range(2):
                pair = 2 * group + n
                plane = both[:, n * LANES : (n + 1) * LANES]
                if pair < 2 and bx > 0:
                    plane = plane + carry[pair]
                if pair >= 4 and bx < 3:
                    carry[pair - 4] = plane
                else:
                    wire_ref[pl.ds(4 * bx + pair, PLANES, stride=WIRE_ROWS), :] = plane
    tail_x, tail_y = tail_distances(last_blocks(pos_x), last_blocks(pos_y))
    product = spline_weight(tail_x) * spline_weight(tail_y)
    tail = dot3(split(last_blocks(waves)), split(product), NT)
    wire_ref[pl.ds(PATCH_ROWS, PLANES, stride=WIRE_ROWS), :] = tail


def pack_weights(w_first, b_first, w_second, b_second, w_out, b_out):
    parts = [
        w_first.transpose(2, 0, 1),
        w_second.transpose(1, 0, 2),
        w_out.transpose(0, 2, 1),
        b_first[None],
        b_second[None],
        b_out[None],
    ]
    basis = np.zeros((2, PLANES // 2, LANES), np.float32)
    basis[:, :, :ZROWS] = cas(np.arange(PLANES), np.arange(ZROWS), PLANES).reshape(2, PLANES // 2, ZROWS)
    parts.append(basis.transpose(1, 0, 2))
    height = sum(part.shape[0] for part in parts)
    total, first = 0.0, 0
    for part in parts:
        after = height - first - part.shape[0]
        total = total + jnp.pad(part, ((first, after), (0, 0), (0, LANES - part.shape[2])))
        first += part.shape[0]
    return total


def atoms_call(ext, left, right, begun, packed):
    f32 = jnp.float32
    return pl.pallas_call(
        atoms_kernel,
        out_shape=(
            jax.ShapeDtypeStruct((4, 4, LANES), f32),
            jax.ShapeDtypeStruct((4, 4, LANES), f32),
            jax.ShapeDtypeStruct((PLANES * WIRE_ROWS, LANES), f32),
        ),
        scratch_shapes=[
            pltpu.VMEM((6, 4, 24, LANES), f32),
            pltpu.VMEM((4, 16, LANES), f32),
            pltpu.VMEM((SPECIES * RADIAL, 16, LANES), f32),
            pltpu.VMEM((3, 32, LANES), f32),
            pltpu.VMEM((8, LANES), f32),
        ],
        compiler_params=pltpu.CompilerParams(vmem_limit_bytes=VMEM_BYTES),
        name="atoms",
    )(ext, left, right, begun, packed)


def filter_kernel(terms_ref, squares_ref, row_ref, out_ref):
    half = NX // 2
    count = NZ // 4

    def series(square):
        total = None
        for t in range(1, count + 1, 4):
            near = [square + squares_ref[t + n] for n in range(4)]
            parts = [
                (
                    terms_ref[t + n] * near[n + 1] + terms_ref[t + n + 1] * near[n],
                    near[n] * near[n + 1],
                )
                for n in (0, 2)
            ]
            part = (parts[0][0] * parts[1][1] + parts[1][0] * parts[0][1]) / (
                parts[0][1] * parts[1][1]
            )
            total = part if total is None else total + part
        even = square + squares_ref[0]
        extra = terms_ref[0] / jnp.where(even > 0.0, even, 1.0)
        return total + jnp.where(even > 0.0, extra, 0.0)

    square_row, factor_row = row_ref[0:1, :], row_ref[8:9, :]
    middle = row_ref[8:9, half : half + 1]
    edge = series(row_ref[0:8, :] + 0.25) * factor_row * middle
    out_ref[half:, :half] = edge[:, :half]
    first = iota((8, half), 1) == 0
    out_ref[half:, half:] = jnp.where(first, edge[:, half : half + 1], edge[:, :half])
    first_lane = iota((16, half), 1) == 0
    edge = edge[0:1, :half]

    def body(n, _):
        at = pl.multiple_of(n * 16, 16)
        here = at + iota((16, half), 0) == iota((16, half), 1)

        def column(row):
            return jnp.sum(jnp.where(here, row[:, :half], 0.0), axis=1, keepdims=True)

        value = series(square_row[:, :half] + column(square_row)) * factor_row[:, :half] * column(factor_row)
        out_ref[pl.ds(at, 16), :half] = value
        out_ref[pl.ds(at, 16), half:] = jnp.where(first_lane, column(edge), value)
        return 0

    lax.fori_loop(0, half // 16, body, 0)


def filter_tables():
    plane = np.arange(PLANES)[:, None]
    odd = np.arange(1, NZ // 2, 2)
    gaps = np.arange(-(PLANES // 2) + 1, PLANES // 2 + 1)
    window = np.cos(2.0 * np.pi / PLANES * plane * gaps) @ np.cos(
        2.0 * np.pi / NZ * gaps[:, None] * odd
    )
    even = 2 * np.minimum(plane, PLANES - plane)
    wave = np.concatenate([even, np.broadcast_to(odd, (PLANES, odd.size))], axis=1)
    square, factor = axis_factor(wave, NZ)
    count = np.concatenate([np.full((PLANES, 1), float(PLANES)), 2.0 * window], axis=1)
    terms = count * factor / (np.pi * NX * NY * NZ * PLANES)
    return terms.astype(np.float32), square.astype(np.float32)


def filter_call(plane):
    terms, squares = filter_tables()
    square, factor = axis_factor(wave_order(NX), NX)
    row = np.repeat(np.stack([square, factor]), 8, axis=0).astype(np.float32)
    smem = pl.BlockSpec(memory_space=pltpu.SMEM)
    vmem = pl.BlockSpec(memory_space=pltpu.VMEM)
    return pl.pallas_call(
        filter_kernel,
        out_shape=jax.ShapeDtypeStruct((NX // 2 + 8, NY), jnp.float32),
        in_specs=[smem, smem, vmem],
        compiler_params=pltpu.CompilerParams(vmem_limit_bytes=VMEM_BYTES),
        cost_estimate=pl.CostEstimate(flops=20_000_000, bytes_accessed=1 << 20, transcendentals=0),
        name="filter",
    )(
        lax.dynamic_index_in_dim(jnp.asarray(terms), plane, 0, keepdims=False),
        lax.dynamic_index_in_dim(jnp.asarray(squares), plane, 0, keepdims=False),
        row,
    )


def plane_kernel(
    count_x,
    count_y,
    wire_ref,
    filter_ref,
    table_ref,
    out_ref,
    grid_high,
    grid_low,
    result_ref,
    y_high,
    y_low,
    yt_high,
    yt_low,
    x_high,
    x_low,
    xt_high,
    xt_low,
):
    width = x_high.shape[0]

    def fill(high_ref, low_ref, first, value):
        high_ref[first : first + 16, :], low_ref[first : first + 16, :] = split(value)

    def part(name, lanes):
        first, height = TABLE[name]
        return table_ref[first : first + height, :lanes]

    cosine, sine = part("y cos", NY), part("y sin", NY)
    for a in range(32):
        at = slice(a, a + 1)
        fill(y_high, y_low, 16 * a, cosine[at] * part("y cas", NY) + sine[at] * part("y sac", NY))
    cosine, sine = part("x cos", NX), part("x sin", NX)
    plus, minus = part("x cas", NX), part("x sac", NX)
    for x in range(width // 16):
        at = slice(x, x + 1)
        fill(x_high, x_low, 16 * x, cosine * plus[at] + sine * minus[at])
    for name, lanes, high, low in (("yt", NY, yt_high, yt_low), ("xt", width, xt_high, xt_low)):
        cosine, sine = part(name + " cos", lanes), part(name + " sin", lanes)
        plus, minus = part(name + " cas", lanes), part(name + " sac", lanes)
        middle = part(name + " mid", lanes)[0:1]
        for a in range(16):
            at = slice(a, a + 1)
            fill(high, low, 16 * a, cosine[at] * plus + sine[at] * minus)
            value = cosine[at] * minus - sine[at] * plus
            if a == 0:
                value = jnp.where(iota((16, lanes), 0) == 0, middle, value)
            fill(high, low, 256 + 16 * a, value)

    stride = count_y * WIRE_ROWS
    pairs = count_y // 2
    lane = iota((count_x, LANES), 1)
    low_half = lane < 64
    tails = [wire_ref[pl.ds(j * WIRE_ROWS + PATCH_ROWS, count_x, stride=stride), :] for j in range(count_y)]
    own_rows = PATCH_ROWS - 2
    for m in range(pairs):
        before = tails[(2 * m - 1) % count_y]
        between = tails[2 * m]

        def unpacked(x):
            r, h = x // 2, x % 2
            one = wire_ref[pl.ds(2 * m * WIRE_ROWS + r, count_x, stride=stride), :]
            two = wire_ref[pl.ds((2 * m + 1) * WIRE_ROWS + r, count_x, stride=stride), :]
            if h == 0:
                value = jnp.where(low_half, one, pltpu.roll(two, 64, 1))
            else:
                value = jnp.where(low_half, pltpu.roll(one, 64, 1), two)
            first = pltpu.roll(before, (LANES - 3 * x) % LANES, 1) if x else before
            second = pltpu.roll(between, (LANES + 64 - 3 * x) % LANES, 1)
            value = value + jnp.where(lane < 3, first, 0.0)
            return value + jnp.where((lane >= 64) & (lane < 67), second, 0.0)

        for x in range(2 * own_rows):
            value = unpacked(x)
            if x < 3:
                value = value + pltpu.roll(unpacked(x + 2 * own_rows), 1, 0)
            high, low = split(value)
            at = x * count_x
            grid_high[at : at + count_x, m * LANES : (m + 1) * LANES] = high
            grid_low[at : at + count_x, m * LANES : (m + 1) * LANES] = low

    step = split(dot3((grid_high[...], grid_low[...]), (y_high[...], y_low[...])))
    spectrum = dot3((xt_high[...], xt_low[...]), step)
    half = NX // 2
    upper = filter_ref[:half, :]
    lower = jnp.where(iota((half, NY), 0) == 0, filter_ref[half : half + 1, :], upper)
    spectrum = jnp.concatenate([spectrum[:half] * upper, spectrum[half:] * lower], axis=0)
    mean = spectrum[0:1, 0:1]
    first = (iota((8, NX), 0) == 0) & (iota((8, NX), 1) == 0)
    spectrum = jnp.concatenate([jnp.where(first, 0.0, spectrum[:8]), spectrum[8:]], axis=0)
    step = split(dot3((x_high[...], x_low[...]), split(spectrum)))
    result_ref[...] = dot3(step, (yt_high[...], yt_low[...]))

    def result_row(x, m):
        here = x % (2 * own_rows)
        value = result_ref[here * count_x : (here + 1) * count_x, m * LANES : (m + 1) * LANES]
        return pltpu.roll(value, count_x - 1, 0) if x >= 2 * own_rows else value

    for j in range(count_y):
        m = j // 2
        for r in range(PATCH_ROWS):
            even, odd = result_row(2 * r, m), result_row(2 * r + 1, m)
            if j % 2 == 0:
                value = jnp.where(low_half, even, pltpu.roll(odd, 64, 1))
            else:
                value = jnp.where(low_half, pltpu.roll(even, 64, 1), odd)
            out_ref[pl.ds(j * WIRE_ROWS + r, count_x, stride=stride), :] = value
        after = (j + 1) % count_y
        m = after // 2
        tail = jnp.where(lane == LANES - 1, mean, 0.0)
        for x in range(2 * PATCH_ROWS):
            value = result_row(x, m)
            shift = (3 * x - 64 * (after % 2)) % LANES
            if shift:
                value = pltpu.roll(value, shift, 1)
            tail = jnp.where((lane >= 3 * x) & (lane < 3 * x + 3), value, tail)
        out_ref[pl.ds(j * WIRE_ROWS + PATCH_ROWS, count_x, stride=stride), :] = tail


def table_layout():
    heights = {"y cos": 32, "y sin": 32, "y cas": 16, "y sac": 16}
    heights.update({"x cos": 16, "x sin": 16, "x cas": 32, "x sac": 32})
    for name in ("yt", "xt"):
        heights.update({name + " cos": 16, name + " sin": 16, name + " cas": 16, name + " sac": 16, name + " mid": 8})
    layout, first = {}, 0
    for name, height in heights.items():
        layout[name] = (first, height)
        first += height
    return layout, first


TABLE, TABLE_ROWS = table_layout()


def plane_tables(count_x):
    wave, cell = wave_order(NY), np.arange(NY)
    own = np.arange(NX // count_x)
    place = (own[:, None] + (NX // count_x) * np.arange(count_x)).reshape(-1)
    out = np.zeros((TABLE_ROWS, NX), np.float32)

    def put(name, rows, lanes):
        angle = 2.0 * np.pi / NX * (np.outer(rows, lanes) % NX)
        cosine, sine = np.cos(angle), np.sin(angle)
        value = {"cos": cosine, "sin": sine, "cas": cosine + sine, "sac": cosine - sine, "mid": cosine}
        first = TABLE[name][0]
        out[first : first + len(rows), : len(lanes)] = value[name[-3:]]

    sixteen = np.arange(16)
    for kind in ("cos", "sin"):
        put("y " + kind, 16 * np.arange(32), wave)
        put("x " + kind, (NX // count_x) * np.arange(count_x), wave)
        put("yt " + kind, 16 * sixteen, cell)
        put("xt " + kind, 16 * sixteen, place)
    for kind in ("cas", "sac"):
        put("y " + kind, sixteen, wave)
        put("x " + kind, own, wave)
        put("yt " + kind, sixteen, cell)
        put("xt " + kind, sixteen, place)
    put("yt mid", np.array([NY // 2]), cell)
    put("xt mid", np.array([NX // 2]), place)
    return out


def plane_call(wire, table, tables, count_x, count_y):
    return pl.pallas_call(
        functools.partial(plane_kernel, count_x, count_y),
        out_shape=jax.ShapeDtypeStruct((PLANES * WIRE_ROWS, LANES), jnp.float32),
        scratch_shapes=[
            pltpu.VMEM((NX, NY), jnp.bfloat16),
            pltpu.VMEM((NX, NY), jnp.bfloat16),
            pltpu.VMEM((NX, NY), jnp.float32),
            *[pltpu.VMEM((NY, NY), jnp.bfloat16)] * 4,
            *[pltpu.VMEM((NX, NX), jnp.bfloat16)] * 2,
            *[pltpu.VMEM((NX, NX), jnp.bfloat16)] * 2,
        ],
        compiler_params=pltpu.CompilerParams(vmem_limit_bytes=VMEM_BYTES),
        name="plane",
    )(wire, table, tables)


def force_kernel(
    wire_ref, place_ref, short_ref, charge_ref, basis_ref, energy_ref, force_ref, rows_ref
):
    for c in range(3):
        for bz in range(4):
            rows_ref[c, 4 * bz : 4 * bz + 4, :] = place_ref[c, bz, 1:5, :]
    pos_x, pos_y, pos_z = [row_vector(rows_ref[c]) for c in range(3)]
    planes = jnp.concatenate(
        [wire_ref[pl.ds(r, PLANES, stride=WIRE_ROWS), :] for r in range(WIRE_ROWS)], axis=1
    )
    basis = basis_ref[...]
    layers = dot3(split(basis), split(planes))
    mean = lax.dot_general(
        basis,
        planes[:, PATCH_ROWS * LANES :],
        NN,
        precision=lax.Precision.HIGHEST,
        preferred_element_type=jnp.float32,
    )[:, LANES - 1 :]
    high, low = split(layers)
    high, low = high.astype(jnp.float32), low.astype(jnp.float32)
    rest = jnp.zeros((LANES - 3 * ZPAD, layers.shape[1]), jnp.float32)
    columns = jnp.concatenate([high, high, low, rest], axis=0).T.astype(jnp.bfloat16)

    def fold(value):
        out = value[0:8]
        for n in range(1, value.shape[0] // 8):
            out = out + value[8 * n : 8 * n + 8]
        return out

    def z_table(weight, slope):
        high, low = split(jnp.concatenate([weight, slope], axis=1))
        high, low = high.astype(jnp.float32), low.astype(jnp.float32)
        rest = jnp.zeros((LANES - 3 * ZPAD, high.shape[1]), jnp.float32)
        return jnp.concatenate([high, low, high, rest], axis=0).astype(jnp.bfloat16)

    last_x, last_y, last_z = [last_blocks(v) for v in (pos_x, pos_y, pos_z)]
    size = last_x.shape[1]
    layer = (iota((ZPAD, size), 1) // SLOTS) % ZBLOCKS
    last_distance = (iota((ZPAD, size), 0) - 8 * layer - 1).astype(jnp.float32) - 8.0 * last_z
    field = dot(columns[PATCH_ROWS * LANES :, :], z_table(*spline_both(last_distance)))
    here, slope = field[:, :size], field[:, size:]
    tail_x, tail_y = tail_distances(last_x, last_y)
    (tail_x, tail_sx), (tail_y, tail_sy) = spline_both(tail_x), spline_both(tail_y)
    here_y = here * tail_y
    tails = [
        jnp.sum(fold(v), axis=0, keepdims=True)
        for v in (here_y * tail_x, here_y * tail_sx, here * tail_sy * tail_x, slope * tail_y * tail_x)
    ]
    last_lanes = iota((1, LANES), 1) >= LANES - SLOTS

    def tail_of(n, bx, bz):
        at = bx * ZBLOCKS + bz
        half = tails[n][:, (at // 8) * LANES : (at // 8 + 1) * LANES]
        shift = (LANES - SLOTS * (at % 8 + 1)) % LANES
        return jnp.where(last_lanes, pltpu.roll(half, shift, 1) if shift else half, 0.0)

    per = 4 * LANES
    for bx in range(4):
        cut = slice(bx * per, (bx + 1) * per)
        ux, uy = 8.0 * pos_x[:, cut], pos_y[:, cut]
        weight_z, slope_z = spline_both(z_distance(pos_z[:, cut]))
        table = z_table(weight_z, slope_z)
        weight_y, slope_y = spline_both(y_distance(uy, (64, per), iota((64, per), 0)))
        weight_x, slope_x = spline_both((iota((16, per), 0) - 1).astype(jnp.float32) - ux)
        zero = jnp.zeros((8, per), jnp.float32)
        total = [fold(weight_z * mean), zero, zero, fold(slope_z * mean)]
        for pair in range(6):
            r = 4 * bx + pair
            field = dot(columns[r * LANES : (r + 1) * LANES, :], table)
            for h in range(2):
                x = 2 * pair + h
                here = field[64 * h : 64 * h + 64, :per]
                slope = field[64 * h : 64 * h + 64, per:]
                plain = fold(here * weight_y)
                along_y = fold(here * slope_y)
                along_z = fold(slope * weight_y)
                wx, sx = weight_x[x : x + 1, :], slope_x[x : x + 1, :]
                total[0] = total[0] + plain * wx
                total[1] = total[1] + plain * sx
                total[2] = total[2] + along_y * wx
                total[3] = total[3] + along_z * wx
        sums = [jnp.sum(t, axis=0, keepdims=True) for t in total]
        for bz in range(4):
            at = slice(bz * LANES, (bz + 1) * LANES)
            charge = charge_ref[bz, bx : bx + 1, :]
            found = [sums[n][:, at] + tail_of(n, bx, bz) for n in range(4)]
            energy_ref[bz, bx : bx + 1, :] = short_ref[bz, bx : bx + 1, :] + 0.5 * charge * found[0]
            for c in range(3):
                force_ref[c, bz, bx : bx + 1, :] = -charge * found[1 + c]


def force_call(wire, place, short, charge):
    basis = np.zeros((ZPAD, PLANES))
    basis[:ZROWS] = cas(np.arange(ZROWS), np.arange(PLANES), PLANES)
    return pl.pallas_call(
        force_kernel,
        out_shape=(
            jax.ShapeDtypeStruct((4, 4, LANES), jnp.float32),
            jax.ShapeDtypeStruct((3, 4, 4, LANES), jnp.float32),
        ),
        scratch_shapes=[pltpu.VMEM((3, 16, LANES), jnp.float32)],
        compiler_params=pltpu.CompilerParams(vmem_limit_bytes=VMEM_BYTES),
        name="force",
    )(wire, place, short, charge, basis.astype(np.float32))


def ring(size):
    up = [(i, (i + 1) % size) for i in range(size)]
    return up, [(j, i) for i, j in up]


def exchange(wire):
    moved = lax.all_to_all(
        wire.reshape(PLANES, 1, WIRE_ROWS * LANES), ("gx", "gy"), split_axis=0, concat_axis=0, tiled=True
    )
    return moved.reshape(PLANES * WIRE_ROWS, LANES)


def shards(atom_cells, atom_frac, species, *weights):
    count_x, count_y = lax.axis_size("gx"), lax.axis_size("gy")
    assert count_x * count_y == PLANES and atom_cells.shape[1:] == (4, 4, LANES)
    shape = (4,) + species.shape
    is_kind = lax.broadcasted_iota(jnp.int32, shape, 0) == 3
    last = ((0, 1), (0, 0), (0, 0), (0, 0))
    whole = jnp.where(is_kind, jnp.broadcast_to(species, shape), jnp.pad(atom_cells & (BLOCK - 1), last))
    own = (whole.astype(jnp.float32) + jnp.pad(atom_frac, last)) * jnp.where(is_kind, 1.0, 1.0 / BLOCK)
    packed = pack_weights(*weights)
    up, down = ring(count_x)
    before = lax.ppermute(own[:, :, 3:4, :], "gx", up)
    after = lax.ppermute(own[:, :, 0:1, :], "gx", down)
    begun = column_pairs_call(own)
    before, after, packed, begun = lax.optimization_barrier((before, after, packed, begun))
    ext = jnp.concatenate([before, own, after, after, after], axis=2)
    up, down = ring(count_y)
    left = lax.ppermute(ext, "gy", up)
    right = lax.ppermute(ext, "gy", down)
    tables = plane_tables(count_x)
    table = filter_call(lax.axis_index(("gx", "gy")))
    begun = first_pairs_call(ext, begun)
    short, charge, wire = atoms_call(ext, left, right, begun, packed)
    wire = exchange(wire)
    wire = plane_call(wire, table, tables, count_x, count_y)
    wire = exchange(wire)
    energy, force = force_call(wire, ext, short, charge)
    return energy, force, charge


def solution(mesh):
    atoms = P(None, "gx", "gy")
    vectors = P(None, None, "gx", "gy")
    return jax.shard_map(
        shards,
        mesh=mesh,
        in_specs=(vectors, vectors, atoms, P(), P(), P(), P(), P(), P()),
        out_specs=(atoms, vectors, atoms),
        check_vma=False,
    )
```
